32 devices in a mesh: req: 16 (over z, y, core), tp: 2 (over x).
Axes of the slice: x: 2, y: 2, z: 4, core: 2. Of those that a mesh axis runs over, the one named last changes fastest.
Arguments:
- hidden_in: bfloat16 [2048, 5120], P('req', 'tp'), may hold values from -6 to 6
- norm_gain: bfloat16 [5120], P('tp'), may hold values from 0.099609375 to 1.8984375
- q_weight: bfloat16 [5120, 3072], P(None, 'tp'), may hold values from -0.078125 to 0.078125
- q_bias: bfloat16 [3072], P('tp'), may hold values from -4 to 4
- k_weight: bfloat16 [5120, 1024], P(None, 'tp'), may hold values from -0.125 to 0.125
- k_bias: bfloat16 [1024], P('tp'), may hold values from -5 to 5
- v_weight: bfloat16 [5120, 1024], P(None, 'tp'), may hold values from -0.3125 to 0.3125
- v_bias: bfloat16 [1024], P('tp'), may hold values from -10 to 10
- o_weight: bfloat16 [3072, 5120], P('tp'), may hold values from -0.3125 to 0.3125
- prefix_kv: bfloat16 [16384, 2, 1024], P('req', None, 'tp'), as said below
- suffix_len: int32 [16], P('req'), may hold values from 18 to 128, as said below
- req_prefix: int32 [16], P('req'), may hold values from 0 to 3, as said below
- block_owner: int32 [16], replicated, may hold values from 0 to 15, each once
Outputs:
- attn_out: bfloat16 [2048, 5120], P('req', 'tp')
The draws below stay inside these ranges and needn't reach their ends.
Inputs may be any that keep to these rules, and one draw needn't show every extreme that they name: `suffix_len`: suffix tokens of each request; some request has exactly 128 and some exactly 18. `req_prefix`: every prefix is continued by exactly 4 requests. Block j of prefix p is held by req index block_owner[p * 4 + j]; each req index holds one block. `prefix_kv`: cached keys already carry the rotary embedding of their prefix positions.
All inputs are finite; a program needn't handle non-finite values.
Results may differ from the reference program's by a relative error of at most 0.022.
Values may be sent and summed in bfloat16 or wider, within the bound.
A program may use at most 192 MiB of HBM per device.

```python
import jax
import jax.numpy as jnp
from jax import lax

D = 5120
HD = 128
KVH = 8
QH = 24
NPREF = 4
SUF = 128
PBLK = 1024
REQS = 16
OWN = 4
PREF = 4096
N_TP = 2


def draw_prefix_kv(key, part):
    key_keys, key_values = jax.random.split(jax.random.fold_in(key, 11), 2)
    rows = REQS * PBLK
    width = KVH * HD
    keys = jax.random.normal(key_keys, (rows, width), jnp.float32) * 1.5
    values = jax.random.normal(key_values, (rows, width), jnp.float32) * 4.0
    return jnp.stack([keys, values], axis=1).astype(jnp.bfloat16)


def draw_suffix_len(key, part):
    key_draw, key_rank = jax.random.split(jax.random.fold_in(key, 23))
    shortest = max(1, SUF // 7)
    lengths = jax.random.randint(key_draw, (REQS,), shortest, SUF + 1)
    ranking = jax.random.permutation(key_rank, REQS)
    lengths = lengths.at[ranking[0]].set(SUF)
    lengths = lengths.at[ranking[1]].set(shortest)
    return lengths.astype(jnp.int32)


def draw_req_prefix(key, part):
    shuffled = jax.random.permutation(jax.random.fold_in(key, 37), REQS)
    return (shuffled % NPREF).astype(jnp.int32)


def levels(rng, extent, cuts, least, largest):
    loudness, own = 1.0, jax.random.fold_in(rng, 6)
    for position, shards_of in cuts:
        draws = jnp.exp(jax.random.uniform(jax.random.fold_in(own, position), (shards_of,), jnp.float32, least / len(cuts), largest / len(cuts)))
        loudness = loudness * jnp.repeat(draws, extent[position] // shards_of).reshape([-1 if axis == position else 1 for axis in range(len(extent))])
    return loudness


def centred(rng, shape, scale, limit, shards=(), held_as=jnp.bfloat16):
    factor_of = levels(rng, shape, shards, -0.22, 0.18) if shards else 1.0
    drawn = jax.random.normal(rng, shape, jnp.float32) * scale * factor_of
    return jnp.minimum(jnp.maximum(drawn, -limit), limit).astype(held_as)


def setup_inputs(seed: int = 0) -> dict:
    splits = jax.random.split(jax.random.key(seed), 14)
    hidden_in = centred(splits[0], (REQS * SUF, D), 1.0, 6.0, ((0, 16), (1, 2)))
    norm_gain = jnp.clip(1.0 + 0.18 * jax.random.normal(splits[1], (D,), jnp.float32), 0.099609375, 1.8984375).astype(jnp.bfloat16)
    q_weight = centred(splits[2], (D, QH * HD), D ** -0.5, 0.078125, ((1, 2),))
    q_bias = centred(splits[3], (QH * HD,), 0.5, 4.0, ((0, 2),))
    k_weight = centred(splits[4], (D, KVH * HD), (D // 2) ** -0.5, 0.125, ((1, 2),))
    k_bias = centred(splits[5], (KVH * HD,), 1.0, 5.0, ((0, 2),))
    v_weight = centred(splits[6], (D, KVH * HD), (D // 16) ** -0.5, 0.3125, ((1, 2),))
    v_bias = centred(splits[7], (KVH * HD,), 2.0, 10.0, ((0, 2),))
    o_weight = centred(splits[8], (QH * HD, D), (QH * HD // 9) ** -0.5, 0.3125, ((0, 2),))
    prefix_kv = draw_prefix_kv(jax.random.fold_in(splits[13], 71), 0)
    suffix_len = draw_suffix_len(jax.random.fold_in(splits[13], 71), 0)
    req_prefix = draw_req_prefix(jax.random.fold_in(splits[13], 71), 0)
    block_owner = jax.random.permutation(splits[12], REQS).astype(jnp.int32)
    return dict(hidden_in=hidden_in, norm_gain=norm_gain, q_weight=q_weight, q_bias=q_bias, k_weight=k_weight, k_bias=k_bias, v_weight=v_weight, v_bias=v_bias, o_weight=o_weight, prefix_kv=prefix_kv, suffix_len=suffix_len, req_prefix=req_prefix, block_owner=block_owner)


THETA = 1000000.0
EPSILON = 1e-06

def rotate(heads, positions):
    half = HD // 2
    freqs = THETA ** (-(jnp.arange(half, dtype=jnp.float32) * 2.0) / HD)
    angles = positions.astype(jnp.float32)[:, None] * freqs[None, :]
    cosine = jnp.cos(angles)[:, None, :]
    sine = jnp.sin(angles)[:, None, :]
    first = heads[..., :half]
    second = heads[..., half:]
    return jnp.concatenate([first * cosine - second * sine, second * cosine + first * sine], axis=-1)

def reference(hidden_in, norm_gain, q_weight, q_bias, k_weight, k_bias, v_weight, v_bias, o_weight, prefix_kv, suffix_len, req_prefix, block_owner):
    group = QH // KVH
    tokens = hidden_in.astype(jnp.float32)
    meansq = lax.optimization_barrier(jnp.mean(tokens * tokens, axis=-1, keepdims=True))
    normed = (tokens * lax.rsqrt(meansq + EPSILON) * norm_gain.astype(jnp.float32)).astype(jnp.bfloat16)
    positions = PREF + jnp.arange(SUF, dtype=jnp.int32)
    queries = jnp.dot(normed, q_weight, preferred_element_type=jnp.float32) + q_bias.astype(jnp.float32)
    queries = rotate(queries.reshape(REQS, SUF, QH, HD), positions).astype(jnp.bfloat16)
    keys = jnp.dot(normed, k_weight, preferred_element_type=jnp.float32) + k_bias.astype(jnp.float32)
    keys = rotate(keys.reshape(REQS, SUF, KVH, HD), positions).astype(jnp.bfloat16)
    values = jnp.dot(normed, v_weight, preferred_element_type=jnp.float32) + v_bias.astype(jnp.float32)
    values = values.astype(jnp.bfloat16).reshape(REQS, SUF, KVH, HD)
    blocks = prefix_kv.reshape(REQS, PBLK, 2, KVH * HD)
    slot_index = jnp.arange(SUF, dtype=jnp.int32)
    key_index = jnp.arange(PREF + SUF, dtype=jnp.int32)
    allowed = key_index[None, :] <= (PREF + slot_index)[:, None]

    def one_request(items):
        query, key_suffix, value_suffix, which = items
        owners = lax.dynamic_slice_in_dim(block_owner, (which * OWN).astype(jnp.int32), OWN)
        cached = jnp.take(blocks, owners, axis=0).reshape(PREF, 2, KVH, HD)
        all_keys = jnp.concatenate([cached[:, 0], key_suffix], axis=0)
        all_values = jnp.concatenate([cached[:, 1], value_suffix], axis=0)
        grouped = query.reshape(SUF, KVH, group, HD)
        scores = jnp.einsum('sghd,kgd->sghk', grouped.astype(jnp.float32), all_keys.astype(jnp.float32)) * HD ** (-0.5)
        scores = jnp.where(allowed[:, None, None, :], scores, -jnp.inf)
        peak = lax.optimization_barrier(jnp.max(scores, axis=-1, keepdims=True))
        weights = jnp.exp(scores - peak)
        total = lax.optimization_barrier(jnp.sum(weights, axis=-1))
        mixed = jnp.einsum('sghk,kgd->sghd', weights.astype(jnp.bfloat16).astype(jnp.float32), all_values.astype(jnp.float32))
        context = mixed / total[..., None]
        return context.astype(jnp.bfloat16).reshape(SUF, QH * HD)
    context = lax.map(one_request, (queries, keys, values, req_prefix))
    context = context.reshape(REQS * SUF, QH * HD)
    width = QH * HD // N_TP
    pieces = context.reshape(REQS * SUF, N_TP, width).transpose(1, 0, 2)
    weights_grouped = o_weight.reshape(N_TP, width, D)

    def add_group(total, items):
        piece, weight = items
        partial_value = jnp.dot(piece, weight, preferred_element_type=jnp.float32).astype(jnp.bfloat16)
        partial_value = lax.optimization_barrier(partial_value)
        return (total + partial_value.astype(jnp.float32), None)
    summed, unused = lax.scan(add_group, jnp.zeros((REQS * SUF, D), jnp.float32), (pieces, weights_grouped))
    valid = (slot_index[None, :] < suffix_len[:, None]).reshape(REQS * SUF)
    return jnp.where(valid[:, None], summed, jnp.float32(0.0)).astype(jnp.bfloat16)
```

```python
import functools

import jax
import jax.numpy as jnp
from jax import lax
from jax.experimental import pallas as pl
from jax.experimental.pallas import tpu as pltpu
from jax.sharding import PartitionSpec as P

HD = 128
NPREF = 4
OUTER = 4
CHUNKS = 2

THETA = 1000000.0
EPSILON = 1e-06
LOWEST = -1e30


def rotate(heads, positions):
    half = HD // 2
    freqs = THETA ** (-(jnp.arange(half, dtype=jnp.float32) * 2.0) / HD)
    angles = positions.astype(jnp.float32)[:, None] * freqs[None, :]
    cosine = jnp.cos(angles)[:, None, :]
    sine = jnp.sin(angles)[:, None, :]
    first = heads[..., :half]
    second = heads[..., half:]
    return jnp.concatenate(
        [first * cosine - second * sine, second * cosine + first * sine], axis=-1
    )


def attend_kernel(outer, inner, group, flags, *refs):
    qs, refs = refs[:outer], refs[outer:]
    ks, refs = refs[:inner], refs[inner:]
    vs, refs = refs[:inner], refs[inner:]
    sk, sv, out, lse, qall, acc, peak, total = refs
    rows = qall.shape[1]
    length = rows // group
    scale = HD ** (-0.5)
    nt = (((1,), (1,)), ((), ()))

    for s in range(outer):
        qall[s] = qs[s][0]
    peak[...] = jnp.full_like(peak, LOWEST)
    total[...] = jnp.zeros_like(total)
    acc[...] = jnp.zeros_like(acc)

    scores = lax.dot_general(qall[0], sk[...], nt, preferred_element_type=jnp.float32) * scale
    slot = lax.rem(lax.broadcasted_iota(jnp.int32, scores.shape, 0), length)
    scores = jnp.where(
        lax.broadcasted_iota(jnp.int32, scores.shape, 1) <= slot, scores, -jnp.inf
    )
    top = jnp.max(scores, axis=1, keepdims=True)
    weights = jnp.exp(scores - top)
    peak[0] = top
    total[0] = jnp.sum(weights, axis=1, keepdims=True)
    acc[0] = jnp.dot(weights.astype(jnp.bfloat16), sv[...], preferred_element_type=jnp.float32)

    for k in range(inner):

        @pl.loop(0, outer)
        def _(s, k=k):
            @pl.when(flags[s * inner + k] == 1)
            def _():
                scores = (
                    lax.dot_general(qall[s], ks[k][...], nt, preferred_element_type=jnp.float32)
                    * scale
                )
                old = peak[s]
                top = jnp.maximum(old, jnp.max(scores, axis=1, keepdims=True))
                weights = jnp.exp(scores - top)
                fade = jnp.exp(old - top)
                peak[s] = top
                total[s] = total[s] * fade + jnp.sum(weights, axis=1, keepdims=True)
                acc[s] = acc[s] * fade + jnp.dot(
                    weights.astype(jnp.bfloat16), vs[k][...], preferred_element_type=jnp.float32
                )

    diagonal = lax.broadcasted_iota(jnp.int32, (length, length), 0) == lax.broadcasted_iota(
        jnp.int32, (length, length), 1
    )
    for s in range(outer):
        whole = total[s]
        some = whole > 0.0
        safe = jnp.where(some, whole, 1.0)
        out[s, 0] = (acc[s] / safe).astype(jnp.bfloat16)
        column = jnp.where(some, peak[s] + jnp.log(safe), LOWEST)
        for h in range(group):
            part = jnp.broadcast_to(column[h * length : (h + 1) * length], (length, length))
            lse[s, 0, h : h + 1, :] = jnp.sum(
                jnp.where(diagonal, part, 0.0), axis=0, keepdims=True
            )


def attend(flags, qs, kvs, own_keys, own_values, group, heads):
    outer, inner = len(qs), len(kvs)
    rows = qs[0].shape[1]
    length = rows // group
    block = kvs[0].shape[0]
    one = pl.BlockSpec((1, rows, HD), lambda g, f: (g, 0, 0))
    key_of = pl.BlockSpec((block, HD), lambda g, f: (0, g))
    value_of = pl.BlockSpec((block, HD), lambda g, f: (0, heads + g))
    suffix = pl.BlockSpec((length, HD), lambda g, f: (0, g))
    work = heads * inner * rows * block * HD * 4
    return pl.pallas_call(
        functools.partial(attend_kernel, outer, inner, group),
        grid_spec=pltpu.PrefetchScalarGridSpec(
            num_scalar_prefetch=1,
            grid=(heads,),
            in_specs=[one] * outer + [key_of] * inner + [value_of] * inner + [suffix] * 2,
            out_specs=[
                pl.BlockSpec((outer, 1, rows, HD), lambda g, f: (0, g, 0, 0)),
                pl.BlockSpec((outer, 1, group, length), lambda g, f: (0, g, 0, 0)),
            ],
            scratch_shapes=[
                pltpu.VMEM((outer, rows, HD), jnp.bfloat16),
                pltpu.VMEM((outer, rows, HD), jnp.float32),
                pltpu.VMEM((outer, rows, 1), jnp.float32),
                pltpu.VMEM((outer, rows, 1), jnp.float32),
            ],
        ),
        out_shape=[
            jax.ShapeDtypeStruct((outer, heads, rows, HD), jnp.bfloat16),
            jax.ShapeDtypeStruct((outer, heads, group, length), jnp.float32),
        ],
        compiler_params=pltpu.CompilerParams(vmem_limit_bytes=40 * 1024 * 1024),
        cost_estimate=pl.CostEstimate(
            flops=2 * work,
            bytes_accessed=heads * inner * block * HD * 4,
            transcendentals=heads * inner * rows * block,
        ),
        name="attend",
    )(flags, *qs, *kvs, *kvs, own_keys, own_values)


def shards(
    hidden_in,
    norm_gain,
    q_weight,
    q_bias,
    k_weight,
    k_bias,
    v_weight,
    v_bias,
    o_weight,
    prefix_kv,
    suffix_len,
    req_prefix,
    block_owner,
):
    length, width = hidden_in.shape
    devices = lax.axis_size("req")
    tps = lax.axis_size("tp")
    owned = devices // NPREF
    block = prefix_kv.shape[0]
    prefix_len = block * owned
    kv_heads = k_weight.shape[1] // HD
    q_heads = q_weight.shape[1] // HD
    group = q_heads // kv_heads
    outer = OUTER
    inner = devices // outer
    chunks = min(CHUNKS, kv_heads)
    heads = kv_heads // chunks
    me = lax.axis_index("req")
    mine = lax.axis_index("tp")

    def swap_tp(x, k):
        return lax.ppermute(x, "tp", [(r, r ^ k) for r in range(tps)])

    def swap_req(x, k):
        return lax.ppermute(x, "req", [(r, r ^ k) for r in range(devices)])

    pieces = [hidden_in] + [swap_tp(hidden_in, k) for k in range(1, tps)]
    gains = [norm_gain] + [swap_tp(norm_gain, k) for k in range(1, tps)]

    held = []
    span = heads * HD
    for c in range(chunks):
        part = prefix_kv[:, :, c * span : (c + 1) * span].reshape(block, 2 * span)
        have = {0: part}
        bit = inner // 2
        while bit:
            have.update({k ^ bit: swap_req(x, bit) for k, x in list(have.items())})
            bit //= 2
        held.append([have[k] for k in range(inner)])

    prefix_of = lax.all_gather(req_prefix, "req", axis=0, tiled=True)
    position = jnp.arange(devices, dtype=jnp.int32)
    holds = jnp.zeros((devices,), jnp.int32).at[block_owner].set(position // owned)
    slots = (me // inner ^ jnp.arange(outer, dtype=jnp.int32)) * inner + me % inner
    blocks = me // inner * inner + (me % inner ^ jnp.arange(inner, dtype=jnp.int32))
    flags = (prefix_of[slots][:, None] == holds[blocks][None, :]).astype(jnp.int32).reshape(-1)

    def ordered(parts, axis):
        out = jnp.concatenate(parts, axis=axis)
        for first in range(1, tps):
            order = [parts[first ^ k] for k in range(tps)]
            out = jnp.where(mine == first, jnp.concatenate(order, axis=axis), out)
        return out

    tokens = ordered(pieces, 1).astype(jnp.float32)
    gain = ordered(gains, 0)
    meansq = jnp.mean(tokens * tokens, axis=-1, keepdims=True)
    normed = (tokens * lax.rsqrt(meansq + EPSILON) * gain.astype(jnp.float32)).astype(jnp.bfloat16)
    positions = prefix_len + jnp.arange(length, dtype=jnp.int32)
    queries = jnp.dot(normed, q_weight, preferred_element_type=jnp.float32) + q_bias.astype(
        jnp.float32
    )
    queries = rotate(queries.reshape(length, q_heads, HD), positions).astype(jnp.bfloat16)
    queries = queries.transpose(1, 0, 2).reshape(kv_heads, group * length, HD)
    keys = jnp.dot(normed, k_weight, preferred_element_type=jnp.float32) + k_bias.astype(
        jnp.float32
    )
    keys = rotate(keys.reshape(length, kv_heads, HD), positions).astype(jnp.bfloat16)
    keys = keys.reshape(length, kv_heads * HD)
    values = jnp.dot(normed, v_weight, preferred_element_type=jnp.float32) + v_bias.astype(
        jnp.float32
    )
    values = values.astype(jnp.bfloat16)

    asked = []
    for c in range(chunks):
        own = queries[c * heads : (c + 1) * heads]
        asked.append([own] + [swap_req(own, s * inner) for s in range(1, outer)])
    mixed = []
    for c in range(chunks):
        cols = slice(c * span, (c + 1) * span)
        out, lse = attend(
            flags, asked[c], held[c], keys[:, cols], values[:, cols], group, heads
        )
        outs = [out[0]] + [swap_req(out[s], s * inner) for s in range(1, outer)]
        lses = [lse[0]] + [swap_req(lse[s], s * inner) for s in range(1, outer)]
        top = functools.reduce(jnp.maximum, lses)
        shares = [jnp.exp(x - top) for x in lses]
        whole = functools.reduce(jnp.add, shares)
        total = 0.0
        for x, share in zip(outs, shares):
            part = x.reshape(heads * group, length, HD).astype(jnp.float32)
            total = total + part * (share / whole).reshape(heads * group, length, 1)
        mixed.append(total.astype(jnp.bfloat16).transpose(1, 0, 2).reshape(length, -1))
    context = jnp.concatenate(mixed, axis=1)
    partial_value = jnp.dot(context, o_weight, preferred_element_type=jnp.float32).astype(
        jnp.bfloat16
    )

    def columns(k):
        return lax.dynamic_slice_in_dim(partial_value, (mine ^ k) * width, width, 1)

    summed = columns(0).astype(jnp.float32)
    for k in range(1, tps):
        summed = summed + swap_tp(columns(k), k).astype(jnp.float32)
    valid = jnp.arange(length, dtype=jnp.int32) < suffix_len[0]
    return jnp.where(valid[:, None], summed, jnp.float32(0.0)).astype(jnp.bfloat16)


def solution(mesh):
    placed = (
        P("req", "tp"),
        P("tp"),
        P(None, "tp"),
        P("tp"),
        P(None, "tp"),
        P("tp"),
        P(None, "tp"),
        P("tp"),
        P("tp", None),
        P("req", None, "tp"),
        P("req"),
        P("req"),
        P(),
    )
    return jax.shard_map(
        shards, mesh=mesh, in_specs=placed, out_specs=P("req", "tp"), check_vma=False
    )
```

```python
import functools

import jax
import jax.numpy as jnp
import numpy as np
from jax import lax
from jax.experimental import pallas as pl
from jax.experimental.pallas import tpu as pltpu
from jax.sharding import PartitionSpec as P

HD = 128
NPREF = 4
OUTER = 4
PAD = 8

THETA = 1000000.0
EPSILON = 1e-06
LOWEST = -1e30
MIB = 1024 * 1024
MESH = pl.DeviceIdType.MESH
NT = (((1,), (1,)), ((), ()))


def flip(index, mask):
    bit = 1
    while bit <= mask:
        if mask & bit:
            index = index + bit - 2 * bit * lax.rem(lax.div(index, bit), 2)
        bit *= 2
    return index


def tables(positions):
    freqs = np.float32(THETA) ** (-(np.arange(HD // 2, dtype=np.float32) * 2.0) / HD)
    angles = positions.astype(np.float32)[:, None] * freqs.astype(np.float32)[None, :]
    cosine = np.cos(angles.astype(np.float64)).astype(np.float32)
    sine = np.sin(angles.astype(np.float64)).astype(np.float32)
    return np.concatenate([cosine, cosine], 1), np.concatenate([-sine, sine], 1)


def greet(req, tp, req_masks, tp_masks):
    barrier = pltpu.get_barrier_semaphore()
    for mask in req_masks:
        pl.semaphore_signal(barrier, inc=1, device_id=(flip(req, mask), tp), device_id_type=MESH)
    for mask in tp_masks:
        pl.semaphore_signal(barrier, inc=1, device_id=(req, flip(tp, mask)), device_id_type=MESH)
    pl.semaphore_wait(barrier, len(req_masks) + len(tp_masks))


def to_row(columns, length):
    lane = lax.broadcasted_iota(jnp.int32, (length, length), 1)
    square = jnp.zeros((length, length), jnp.float32)
    for n, column in enumerate(columns):
        square = jnp.where(lane == n, column, square)
    return jnp.transpose(square)[:PAD]


def project_kernel(
    cfg, hidden, gain, bias, cosine, sine, kvs, wq, wk, wv,
    qg, kvg, own_out, own_lse,
    xbuf, gbuf, normed, vq, vk, vv, qbuf,
    wsem, lsem, xsend, xrecv, gsend, grecv, qsend, qrecv, ksend, krecv,
):
    tps, inner, split, slots, kv_heads, group = cfg
    length, width = hidden.shape
    half = kv_heads // split
    req, tp = lax.axis_index("req"), lax.axis_index("tp")
    part = lax.rem(req, split)

    loads = [
        pltpu.make_async_copy(src, dst, wsem.at[n])
        for n, (src, dst) in enumerate(((wq, vq), (wk, vk), (wv, vv)))
    ]
    for load in loads:
        load.start()
    greet(req, tp, sorted(set(slots[1:]) | set(range(1, inner))), range(1, tps))

    swaps = []
    for k in range(1, tps):
        for src, dst, send, recv in ((hidden, xbuf, xsend, xrecv), (gain, gbuf, gsend, grecv)):
            swaps.append(
                pltpu.make_async_remote_copy(
                    src_ref=src,
                    dst_ref=dst.at[tp],
                    send_sem=send.at[k - 1],
                    recv_sem=recv.at[k - 1],
                    device_id=(req, flip(tp, k)),
                    device_id_type=MESH,
                )
            )
    for swap in swaps:
        swap.start()
    blocks = []
    for k in range(inner - 1, 0, -1):
        blocks.append(
            pltpu.make_async_remote_copy(
                src_ref=kvs.at[lax.rem(flip(req, k), split)],
                dst_ref=kvg.at[k],
                send_sem=ksend.at[k - 1],
                recv_sem=krecv.at[k - 1],
                device_id=(flip(req, k), tp),
                device_id_type=MESH,
            )
        )
    for copy in blocks:
        copy.start()
    keep = pltpu.make_async_copy(kvs.at[part], kvg.at[0], lsem.at[0])
    keep.start()
    xbuf[tp] = hidden[...]
    gbuf[tp] = gain[...]
    for swap in swaps:
        swap.wait()

    square = jnp.zeros((length, 1), jnp.float32)
    for t in range(tps):
        tokens = xbuf[t].astype(jnp.float32)
        square = square + jnp.sum(tokens * tokens, axis=1, keepdims=True)
    factor = lax.rsqrt(square / (tps * width) + EPSILON)
    for t in range(tps):
        tokens = xbuf[t].astype(jnp.float32) * factor * gbuf[t][:1]
        normed[:, t * width : (t + 1) * width] = tokens.astype(jnp.bfloat16)

    def rope(x):
        return x * cosine[...] + pltpu.roll(x, HD // 2, 1) * sine[...]

    for load in loads:
        load.wait()
    span = group * HD
    for g in range(kv_heads):
        q = jnp.dot(
            normed[...], vq[:, g * span : (g + 1) * span], preferred_element_type=jnp.float32
        )
        q = q + bias[:, g * span : (g + 1) * span]
        for h in range(group):
            qbuf[g // half, g % half, h * length : (h + 1) * length] = rope(
                q[:, h * HD : (h + 1) * HD]
            ).astype(jnp.bfloat16)
    asks = []
    for n, mask in enumerate(slots[1:]):
        asks.append(
            pltpu.make_async_remote_copy(
                src_ref=qbuf.at[lax.rem(flip(req, mask), split)],
                dst_ref=qg.at[n + 1],
                send_sem=qsend.at[n],
                recv_sem=qrecv.at[n],
                device_id=(flip(req, mask), tp),
                device_id_type=MESH,
            )
        )
    for ask in asks:
        ask.start()
    mine = pltpu.make_async_copy(qbuf.at[part], qg.at[0], lsem.at[1])
    mine.start()

    first = kv_heads * span
    rows = group * length
    slot = lax.rem(lax.broadcasted_iota(jnp.int32, (rows, length), 0), length)
    allowed = lax.broadcasted_iota(jnp.int32, (rows, length), 1) <= slot
    k_all = jnp.dot(normed[...], vk[...], preferred_element_type=jnp.float32)
    k_all = k_all + bias[:, first : first + kv_heads * HD]
    first += kv_heads * HD
    v_all = jnp.dot(normed[...], vv[...], preferred_element_type=jnp.float32)
    v_all = (v_all + bias[:, first : first + kv_heads * HD]).astype(jnp.bfloat16)
    for p in range(split):
        columns = []
        for g in range(half):
            at = (p * half + g) * HD
            keys = rope(k_all[:, at : at + HD]).astype(jnp.bfloat16)
            scores = lax.dot_general(qbuf[p, g], keys, NT, preferred_element_type=jnp.float32)
            scores = jnp.where(allowed, scores * HD ** (-0.5), -jnp.inf)
            top = jnp.max(scores, axis=1, keepdims=True)
            weights = jnp.exp(scores - top)
            total = jnp.sum(weights, axis=1, keepdims=True)
            out = jnp.dot(
                weights.astype(jnp.bfloat16),
                v_all[:, at : at + HD],
                preferred_element_type=jnp.float32,
            )
            own_out[p, g] = (out / total).astype(jnp.bfloat16)
            column = top + jnp.log(total)
            columns += [column[h * length : (h + 1) * length] for h in range(group)]
        own_lse[p] = to_row(columns, length)

    keep.wait()
    mine.wait()
    for copy in asks + blocks:
        copy.wait()


def project(hidden, gain, bias, cosine, sine, kvs, wq, wk, wv, cfg):
    tps, inner, split, slots, kv_heads, group = cfg
    length, width = hidden.shape
    half = kv_heads // split
    rows = group * length
    vmem = pl.BlockSpec(memory_space=pltpu.VMEM)
    hbm = pl.BlockSpec(memory_space=pl.ANY)
    bf16, f32 = jnp.bfloat16, jnp.float32
    dma = pltpu.SemaphoreType.DMA
    return pl.pallas_call(
        functools.partial(project_kernel, cfg),
        in_specs=[vmem] * 5 + [hbm] * 4,
        out_specs=[hbm, hbm, vmem, vmem],
        out_shape=[
            jax.ShapeDtypeStruct((len(slots), half, rows, HD), bf16),
            jax.ShapeDtypeStruct((inner,) + kvs.shape[1:], bf16),
            jax.ShapeDtypeStruct((split, half, rows, HD), bf16),
            jax.ShapeDtypeStruct((split, PAD, length), f32),
        ],
        scratch_shapes=[
            pltpu.VMEM((tps, length, width), bf16),
            pltpu.VMEM((tps,) + gain.shape, f32),
            pltpu.VMEM((length, tps * width), bf16),
            pltpu.VMEM(wq.shape, bf16),
            pltpu.VMEM(wk.shape, bf16),
            pltpu.VMEM(wv.shape, bf16),
            pltpu.VMEM((split, half, rows, HD), bf16),
            dma((3,)),
            dma((2,)),
            dma((tps - 1,)),
            dma((tps - 1,)),
            dma((tps - 1,)),
            dma((tps - 1,)),
            dma((len(slots) - 1,)),
            dma((len(slots) - 1,)),
            dma((inner - 1,)),
            dma((inner - 1,)),
        ],
        compiler_params=pltpu.CompilerParams(
            collective_id=0, has_side_effects=True, vmem_limit_bytes=52 * MIB
        ),
        name="project",
    )(hidden, gain, bias, cosine, sine, kvs, wq, wk, wv)


def attend_kernel(group, flags, qs, ks, vs, out, lse, acc, peak, total):
    slots, _, rows, _ = qs.shape
    inner = ks.shape[0]
    length = rows // group
    scale = HD ** (-0.5)
    head = pl.program_id(0)
    peak[...] = jnp.full_like(peak, LOWEST)
    total[...] = jnp.zeros_like(total)
    acc[...] = jnp.zeros_like(acc)

    @pl.loop(0, slots * inner)
    def _(pair):
        @pl.when(flags[pair] == 1)
        def _():
            s, k = lax.div(pair, inner), lax.rem(pair, inner)
            scores = (
                lax.dot_general(qs[s, 0], ks[k], NT, preferred_element_type=jnp.float32) * scale
            )
            old = peak[s]
            top = jnp.maximum(old, jnp.max(scores, axis=1, keepdims=True))
            weights = jnp.exp(scores - top)
            fade = jnp.exp(old - top)
            peak[s] = top
            total[s] = total[s] * fade + jnp.sum(weights, axis=1, keepdims=True)
            acc[s] = acc[s] * fade + jnp.dot(
                weights.astype(jnp.bfloat16), vs[k], preferred_element_type=jnp.float32
            )

    row = lax.broadcasted_iota(jnp.int32, (PAD, length), 0)

    @pl.loop(0, slots)
    def _(s):
        whole = total[s]
        some = whole > 0.0
        safe = jnp.where(some, whole, 1.0)
        out[s, 0] = (acc[s] / safe).astype(jnp.bfloat16)
        column = jnp.where(some, peak[s] + jnp.log(safe), LOWEST)
        lse[s, 0] = to_row([column[h * length : (h + 1) * length] for h in range(group)], length)


def attend(flags, qg, kvg, group):
    slots, heads, rows, _ = qg.shape
    inner, block, _ = kvg.shape
    length = rows // group
    return pl.pallas_call(
        functools.partial(attend_kernel, group),
        grid_spec=pltpu.PrefetchScalarGridSpec(
            num_scalar_prefetch=1,
            grid=(heads,),
            in_specs=[
                pl.BlockSpec((slots, 1, rows, HD), lambda g, f: (0, g, 0, 0)),
                pl.BlockSpec((inner, block, HD), lambda g, f: (0, 0, g)),
                pl.BlockSpec((inner, block, HD), lambda g, f: (0, 0, heads + g)),
            ],
            out_specs=[
                pl.BlockSpec((slots, 1, rows, HD), lambda g, f: (0, g, 0, 0)),
                pl.BlockSpec((slots, 1, PAD, length), lambda g, f: (0, g, 0, 0)),
            ],
            scratch_shapes=[
                pltpu.VMEM((slots, rows, HD), jnp.float32),
                pltpu.VMEM((slots, rows, 1), jnp.float32),
                pltpu.VMEM((slots, rows, 1), jnp.float32),
            ],
        ),
        out_shape=[
            jax.ShapeDtypeStruct((slots, heads, rows, HD), jnp.bfloat16),
            jax.ShapeDtypeStruct((slots, heads, PAD, length), jnp.float32),
        ],
        compiler_params=pltpu.CompilerParams(vmem_limit_bytes=48 * MIB),
        name="attend",
    )(flags, qg, kvg, kvg)


def finish_kernel(
    cfg, outs, lses, own_out, own_lse, wo,
    result,
    obuf, lbuf, vo, square, context, psend, precv,
    wsem, lsem, osend, orecv, ssend, srecv, xsend, xrecv,
):
    tps, inner, split, slots, kv_heads, group = cfg
    half = kv_heads // split
    length, width = result.shape
    tile = 512 if width % 512 == 0 else width
    req, tp = lax.axis_index("req"), lax.axis_index("tp")
    part = lax.rem(req, split)

    load = pltpu.make_async_copy(wo, vo, wsem.at[0])
    load.start()
    greet(req, tp, slots[1:], range(1, tps))
    copies = []
    for n in range(len(slots) - 1, 0, -1):
        for src, dst, send, recv in ((lses, lbuf, ssend, srecv), (outs, obuf, osend, orecv)):
            copies.append(
                pltpu.make_async_remote_copy(
                    src_ref=src.at[n],
                    dst_ref=dst.at[n],
                    send_sem=send.at[n - 1],
                    recv_sem=recv.at[n - 1],
                    device_id=(flip(req, slots[n]), tp),
                    device_id_type=MESH,
                )
            )
    for copy in copies:
        copy.start()
    keeps = [
        pltpu.make_async_copy(outs.at[0], obuf.at[0], lsem.at[0]),
        pltpu.make_async_copy(lses.at[0], lbuf.at[0], lsem.at[1]),
    ]
    for keep in keeps:
        keep.start()
    for copy in keeps + copies:
        copy.wait()

    square[...] = jnp.zeros_like(square)
    terms = OUTER + 1
    for sub in range(split):
        which = flip(part, sub)
        for g in range(half):
            parts = [lbuf[so * split + sub, g] for so in range(OUTER)]
            own = own_lse[which]
            parts.append(own[g * group : (g + 1) * group])
            parts = [p[:group] for p in parts]
            top = functools.reduce(jnp.maximum, parts)
            shares = [jnp.exp(p - top) for p in parts]
            whole = functools.reduce(jnp.add, shares)
            for j, share in enumerate(shares):
                at = ((sub * half + g) * terms + j) * group
                square[at : at + group] = share / whole
    columns = jnp.transpose(square[...])
    for sub in range(split):
        which = flip(part, sub)
        for g in range(half):
            for h in range(group):
                total = jnp.zeros((length, HD), jnp.float32)
                for j in range(terms):
                    at = ((sub * half + g) * terms + j) * group + h
                    rows = slice(h * length, (h + 1) * length)
                    if j < OUTER:
                        piece = obuf[j * split + sub, g, rows]
                    else:
                        piece = own_out[which, g, rows]
                    total = total + piece.astype(jnp.float32) * columns[:, at : at + 1]
                to = pl.multiple_of(((which * half + g) * group + h) * HD, HD)
                context[:, pl.ds(to, HD)] = total.astype(jnp.bfloat16)

    load.wait()

    def product(target, n):
        at = pl.multiple_of(target * width + n * tile, 128)
        return jnp.dot(
            context[...], vo[:, pl.ds(at, tile)], preferred_element_type=jnp.float32
        ).astype(jnp.bfloat16)

    swaps = []
    for k in range(1, tps):
        for n in range(width // tile):
            psend[k - 1, :, n * tile : (n + 1) * tile] = product(flip(tp, k), n)
        swap = pltpu.make_async_remote_copy(
            src_ref=psend.at[k - 1],
            dst_ref=precv.at[k - 1],
            send_sem=xsend.at[k - 1],
            recv_sem=xrecv.at[k - 1],
            device_id=(req, flip(tp, k)),
            device_id_type=MESH,
        )
        swap.start()
        swaps.append(swap)
    for n in range(width // tile):
        result[:, n * tile : (n + 1) * tile] = product(tp, n).astype(jnp.float32)
    for k, swap in enumerate(swaps):
        swap.wait()
        result[...] += precv[k].astype(jnp.float32)


def finish(outs, lses, own_out, own_lse, wo, cfg):
    tps, inner, split, slots, kv_heads, group = cfg
    length = lses.shape[-1]
    width = wo.shape[1] // tps
    vmem = pl.BlockSpec(memory_space=pltpu.VMEM)
    hbm = pl.BlockSpec(memory_space=pl.ANY)
    bf16, f32 = jnp.bfloat16, jnp.float32
    dma = pltpu.SemaphoreType.DMA
    return pl.pallas_call(
        functools.partial(finish_kernel, cfg),
        in_specs=[hbm, hbm, vmem, vmem, hbm],
        out_specs=vmem,
        out_shape=jax.ShapeDtypeStruct((length, width), f32),
        scratch_shapes=[
            pltpu.VMEM(outs.shape, bf16),
            pltpu.VMEM(lses.shape, f32),
            pltpu.VMEM(wo.shape, bf16),
            pltpu.VMEM((128, length), f32),
            pltpu.VMEM((length, wo.shape[0]), bf16),
            pltpu.VMEM((tps - 1, length, width), bf16),
            pltpu.VMEM((tps - 1, length, width), bf16),
            dma((1,)),
            dma((2,)),
            dma((len(slots) - 1,)),
            dma((len(slots) - 1,)),
            dma((len(slots) - 1,)),
            dma((len(slots) - 1,)),
            dma((tps - 1,)),
            dma((tps - 1,)),
        ],
        compiler_params=pltpu.CompilerParams(
            collective_id=1, has_side_effects=True, vmem_limit_bytes=52 * MIB
        ),
        name="finish",
    )(outs, lses, own_out, own_lse, wo)


def shards(
    hidden_in,
    norm_gain,
    q_weight,
    q_bias,
    k_weight,
    k_bias,
    v_weight,
    v_bias,
    o_weight,
    prefix_kv,
    suffix_len,
    req_prefix,
    block_owner,
):
    length = hidden_in.shape[0]
    devices = lax.axis_size("req")
    tps = lax.axis_size("tp")
    owned = devices // NPREF
    block = prefix_kv.shape[0]
    kv_heads = k_weight.shape[1] // HD
    group = q_weight.shape[1] // k_weight.shape[1]
    inner = devices // OUTER
    split = 2 if kv_heads % 2 == 0 else 1
    half = kv_heads // split
    slots = tuple(so * inner + sub for so in range(OUTER) for sub in range(split))
    cfg = (tps, inner, split, slots, kv_heads, group)
    me = lax.axis_index("req")

    prefixes = [req_prefix]
    for mask in slots[1:]:
        prefixes.append(
            lax.ppermute(req_prefix, "req", [(r, r ^ mask) for r in range(devices)])
        )
    prefixes = jnp.concatenate(prefixes)
    index = jnp.arange(devices, dtype=jnp.int32)
    blocks = me // inner * inner + (me % inner ^ jnp.arange(inner, dtype=jnp.int32))
    holds = jnp.sum(
        jnp.where(block_owner[None, :] == blocks[:, None], (index // owned)[None, :], 0), axis=1
    )
    flags = (prefixes[:, None] == holds[None, :]).astype(jnp.int32).reshape(-1)

    span = half * HD
    kvs = prefix_kv.reshape(block, 2, split, span).transpose(2, 0, 1, 3)
    kvs = kvs.reshape(split, block, 2 * span)
    gain = jnp.broadcast_to(norm_gain.astype(jnp.float32)[None, :], (8, norm_gain.shape[0]))
    bias = jnp.concatenate([q_bias, k_bias, v_bias]).astype(jnp.float32)[None, :]
    cosine, sine = tables(block * owned + np.arange(length))
    qg, kvg, own_out, own_lse = project(
        hidden_in, gain, bias, jnp.asarray(cosine), jnp.asarray(sine), kvs,
        q_weight, k_weight, v_weight, cfg,
    )
    outs, lses = attend(flags, qg, kvg, group)
    summed = finish(outs, lses, own_out, own_lse, o_weight, cfg)
    valid = jnp.arange(length, dtype=jnp.int32) < suffix_len[0]
    return jnp.where(valid[:, None], summed, jnp.float32(0.0)).astype(jnp.bfloat16)


def solution(mesh):
    placed = (
        P("req", "tp"),
        P("tp"),
        P(None, "tp"),
        P("tp"),
        P(None, "tp"),
        P("tp"),
        P(None, "tp"),
        P("tp"),
        P("tp", None),
        P("req", None, "tp"),
        P("req"),
        P("req"),
        P(),
    )
    return jax.shard_map(
        shards, mesh=mesh, in_specs=placed, out_specs=P("req", "tp"), check_vma=False
    )
```

```python
import functools

import jax
import jax.numpy as jnp
import numpy as np
from jax import lax
from jax.experimental import pallas as pl
from jax.experimental.pallas import tpu as pltpu
from jax.sharding import PartitionSpec as P

HD = 128
NPREF = 4
OUTER = 4
PIECES = 2
PAD = 8

THETA = 1000000.0
EPSILON = 1e-06
LOWEST = -1e30
MIB = 1024 * 1024
MESH = pl.DeviceIdType.MESH
NT = (((1,), (1,)), ((), ()))


def flip(index, mask):
    bit = 1
    while bit <= mask:
        if mask & bit:
            index = index + bit - 2 * bit * lax.rem(lax.div(index, bit), 2)
        bit *= 2
    return index


def tables(positions):
    freqs = np.float32(THETA) ** (-(np.arange(HD // 2, dtype=np.float32) * 2.0) / HD)
    angles = positions.astype(np.float32)[:, None] * freqs.astype(np.float32)[None, :]
    cosine = np.cos(angles.astype(np.float64)).astype(np.float32)
    sine = np.sin(angles.astype(np.float64)).astype(np.float32)
    return np.concatenate([cosine, cosine], 1), np.concatenate([-sine, sine], 1)


def heads_of(column, group, length):
    short = length // PIECES
    return [
        jnp.concatenate(
            [column[(p * group + h) * short :][:short] for p in range(PIECES)], axis=0
        )
        for h in range(group)
    ]


def greet(req, tp, req_masks, tp_masks):
    barrier = pltpu.get_barrier_semaphore()
    for mask in req_masks:
        pl.semaphore_signal(barrier, inc=1, device_id=(flip(req, mask), tp), device_id_type=MESH)
    for mask in tp_masks:
        pl.semaphore_signal(barrier, inc=1, device_id=(req, flip(tp, mask)), device_id_type=MESH)
    pl.semaphore_wait(barrier, len(req_masks) + len(tp_masks))


def to_row(columns, length):
    lane = lax.broadcasted_iota(jnp.int32, (length, length), 1)
    square = jnp.zeros((length, length), jnp.float32)
    for n, column in enumerate(columns):
        square = jnp.where(lane == n, column, square)
    return jnp.transpose(square)[:PAD]


def project_kernel(
    cfg, hidden, gain, bias, cosine, sine, prefix, kvs, wq, wk, wv,
    qg, kvg, prefixes, own_out, own_lse,
    xbuf, gbuf, normed, vq, vk, vv, qbuf,
    wsem, lsem, xsend, xrecv, gsend, grecv, qsend, qrecv, ksend, krecv, psend, precv,
):
    tps, inner, split, slots, kv_heads, group = cfg
    length, width = hidden.shape
    half = kv_heads // split
    req, tp = lax.axis_index("req"), lax.axis_index("tp")
    part = lax.rem(req, split)
    short = length // PIECES
    span = group * HD
    step = group * short

    def cached(side, which):
        return pl.multiple_of((side * split + which) * half * HD, HD)

    loads = [
        pltpu.make_async_copy(src, dst, wsem.at[n])
        for n, (src, dst) in enumerate(((wq, vq), (wk, vk), (wv, vv)))
    ]
    for load in loads:
        load.start()
    greet(req, tp, sorted(set(slots[1:]) | set(range(1, inner))), range(1, tps))

    def swap_of(k, piece):
        rows = pl.ds(piece * short, short)
        return pltpu.make_async_remote_copy(
            src_ref=hidden.at[rows],
            dst_ref=xbuf.at[tp, rows],
            send_sem=xsend.at[piece, k - 1],
            recv_sem=xrecv.at[piece, k - 1],
            device_id=(req, flip(tp, k)),
            device_id_type=MESH,
        )

    gains = [
        pltpu.make_async_remote_copy(
            src_ref=gain,
            dst_ref=gbuf.at[tp],
            send_sem=gsend.at[k - 1],
            recv_sem=grecv.at[k - 1],
            device_id=(req, flip(tp, k)),
            device_id_type=MESH,
        )
        for k in range(1, tps)
    ]
    for copy in gains:
        copy.start()
    swaps = [[swap_of(k, piece) for k in range(1, tps)] for piece in range(PIECES)]
    for swap in swaps[0]:
        swap.start()
    blocks = []
    for k in range(inner - 1, 0, -1):
        for side in range(2):
            there = lax.rem(flip(req, k), split)
            blocks.append(
                pltpu.make_async_remote_copy(
                    src_ref=kvs.at[:, pl.ds(cached(side, there), half * HD)],
                    dst_ref=kvg.at[k, :, pl.ds(side * half * HD, half * HD)],
                    send_sem=ksend.at[k - 1, side],
                    recv_sem=krecv.at[k - 1, side],
                    device_id=(flip(req, k), tp),
                    device_id_type=MESH,
                )
            )
    for copy in blocks:
        copy.start()
    for n, mask in enumerate(slots[1:]):
        copy = pltpu.make_async_remote_copy(
            src_ref=prefix,
            dst_ref=prefixes.at[n + 1],
            send_sem=psend.at[n],
            recv_sem=precv.at[n],
            device_id=(flip(req, mask), tp),
            device_id_type=MESH,
        )
        copy.start()
        blocks.append(copy)
    keeps = [pltpu.make_async_copy(prefix, prefixes.at[0], lsem.at[0])]
    for side in range(2):
        keeps.append(
            pltpu.make_async_copy(
                kvs.at[:, pl.ds(cached(side, part), half * HD)],
                kvg.at[0, :, pl.ds(side * half * HD, half * HD)],
                lsem.at[1 + side],
            )
        )
    for keep in keeps:
        keep.start()
    xbuf[tp] = hidden[...]
    gbuf[tp] = gain[...]

    def rope(x, at):
        return x * cosine[at] + pltpu.roll(x, HD // 2, 1) * sine[at]

    asks = []
    for piece in range(PIECES):
        at = slice(piece * short, (piece + 1) * short)
        if piece + 1 < PIECES:
            for swap, later in zip(swaps[piece], swaps[piece + 1]):
                swap.wait_send()
                later.start()
                swap.wait_recv()
        else:
            for swap in swaps[piece]:
                swap.wait()
        if piece == 0:
            for copy in gains:
                copy.wait()
        square = jnp.zeros((short, 1), jnp.float32)
        for t in range(tps):
            tokens = xbuf[t, at].astype(jnp.float32)
            square = square + jnp.sum(tokens * tokens, axis=1, keepdims=True)
        factor = lax.rsqrt(square / (tps * width) + EPSILON)
        for t in range(tps):
            tokens = xbuf[t, at].astype(jnp.float32) * factor * gbuf[t][:1]
            normed[at, t * width : (t + 1) * width] = tokens.astype(jnp.bfloat16)
        if piece == 0:
            loads[0].wait()
        for g in range(kv_heads):
            q = jnp.dot(
                normed[at], vq[:, g * span : (g + 1) * span], preferred_element_type=jnp.float32
            )
            q = q + bias[:, g * span : (g + 1) * span]
            for h in range(group):
                to = piece * step + h * short
                qbuf[g // half, g % half, to : to + short] = rope(
                    q[:, h * HD : (h + 1) * HD], at
                ).astype(jnp.bfloat16)
        rows = pl.ds(piece * step, step)
        for n, mask in enumerate(slots[1:]):
            ask = pltpu.make_async_remote_copy(
                src_ref=qbuf.at[lax.rem(flip(req, mask), split), :, rows],
                dst_ref=qg.at[n + 1, :, rows],
                send_sem=qsend.at[piece, n],
                recv_sem=qrecv.at[piece, n],
                device_id=(flip(req, mask), tp),
                device_id_type=MESH,
            )
            ask.start()
            asks.append(ask)
    mine = pltpu.make_async_copy(qbuf.at[part], qg.at[0], lsem.at[3])
    mine.start()
    for load in loads[1:]:
        load.wait()

    first = kv_heads * span
    rows = group * length
    slot = lax.broadcasted_iota(jnp.int32, (rows, length), 0)
    slot = lax.div(slot, step) * short + lax.rem(slot, short)
    allowed = lax.broadcasted_iota(jnp.int32, (rows, length), 1) <= slot
    k_all = jnp.dot(normed[...], vk[...], preferred_element_type=jnp.float32)
    k_all = k_all + bias[:, first : first + kv_heads * HD]
    first += kv_heads * HD
    v_all = jnp.dot(normed[...], vv[...], preferred_element_type=jnp.float32)
    v_all = (v_all + bias[:, first : first + kv_heads * HD]).astype(jnp.bfloat16)
    for p in range(split):
        columns = []
        for g in range(half):
            at = (p * half + g) * HD
            keys = rope(k_all[:, at : at + HD], slice(None)).astype(jnp.bfloat16)
            scores = lax.dot_general(qbuf[p, g], keys, NT, preferred_element_type=jnp.float32)
            scores = jnp.where(allowed, scores * HD ** (-0.5), -jnp.inf)
            top = jnp.max(scores, axis=1, keepdims=True)
            weights = jnp.exp(scores - top)
            total = jnp.sum(weights, axis=1, keepdims=True)
            out = jnp.dot(
                weights.astype(jnp.bfloat16),
                v_all[:, at : at + HD],
                preferred_element_type=jnp.float32,
            )
            own_out[p, g] = (out / total).astype(jnp.bfloat16)
            column = top + jnp.log(total)
            columns += heads_of(column, group, length)
        own_lse[p] = to_row(columns, length)

    for keep in keeps:
        keep.wait()
    mine.wait()
    for copy in asks + blocks:
        copy.wait()


def project(hidden, gain, bias, cosine, sine, prefix, kvs, wq, wk, wv, cfg):
    tps, inner, split, slots, kv_heads, group = cfg
    length, width = hidden.shape
    half = kv_heads // split
    rows = group * length
    vmem = pl.BlockSpec(memory_space=pltpu.VMEM)
    hbm = pl.BlockSpec(memory_space=pl.ANY)
    bf16, f32 = jnp.bfloat16, jnp.float32
    dma = pltpu.SemaphoreType.DMA
    return pl.pallas_call(
        functools.partial(project_kernel, cfg),
        in_specs=[vmem] * 6 + [hbm] * 4,
        out_specs=[hbm, hbm, hbm, vmem, vmem],
        out_shape=[
            jax.ShapeDtypeStruct((len(slots), half, rows, HD), bf16),
            jax.ShapeDtypeStruct((inner, kvs.shape[0], 2 * half * HD), bf16),
            jax.ShapeDtypeStruct((len(slots),) + prefix.shape, jnp.int32),
            jax.ShapeDtypeStruct((split, half, rows, HD), bf16),
            jax.ShapeDtypeStruct((split, PAD, length), f32),
        ],
        scratch_shapes=[
            pltpu.VMEM((tps, length, width), bf16),
            pltpu.VMEM((tps,) + gain.shape, f32),
            pltpu.VMEM((length, tps * width), bf16),
            pltpu.VMEM(wq.shape, bf16),
            pltpu.VMEM(wk.shape, bf16),
            pltpu.VMEM(wv.shape, bf16),
            pltpu.VMEM((split, half, rows, HD), bf16),
            dma((3,)),
            dma((4,)),
            dma((PIECES, tps - 1)),
            dma((PIECES, tps - 1)),
            dma((tps - 1,)),
            dma((tps - 1,)),
            dma((PIECES, len(slots) - 1)),
            dma((PIECES, len(slots) - 1)),
            dma((inner - 1, 2)),
            dma((inner - 1, 2)),
            dma((len(slots) - 1,)),
            dma((len(slots) - 1,)),
        ],
        compiler_params=pltpu.CompilerParams(
            collective_id=0, has_side_effects=True, vmem_limit_bytes=52 * MIB
        ),
        name="project",
    )(hidden, gain, bias, cosine, sine, prefix, kvs, wq, wk, wv)


def attend_kernel(group, holds, prefixes, qs, ks, vs, out, lse, ones, acc, peak):
    slots, _, rows, _ = qs.shape
    inner, block, _ = ks.shape
    length = rows // group
    scale = HD ** (-0.5)
    base2 = scale * np.log2(np.e)
    peak[...] = jnp.full_like(peak, LOWEST)
    acc[...] = jnp.zeros_like(acc)
    ones[:, :, :HD] = vs[...]
    ones[:, :, HD:] = jnp.ones((inner, block, HD), jnp.bfloat16)

    @pl.loop(0, slots * inner)
    def _(pair):
        s, k = lax.div(pair, inner), lax.rem(pair, inner)

        @pl.when(prefixes[s, 0, 0] == holds[k])
        def _():
            scores = lax.dot_general(qs[s, 0], ks[k], NT, preferred_element_type=jnp.float32)
            old = peak[s]
            top = jnp.maximum(old, jnp.max(scores, axis=1, keepdims=True))
            weights = jnp.exp2((scores - top) * base2)
            fade = jnp.exp2((old - top) * base2)
            peak[s] = top
            acc[s] = acc[s] * fade + jnp.dot(
                weights.astype(jnp.bfloat16), ones[k], preferred_element_type=jnp.float32
            )

    @pl.loop(0, slots)
    def _(s):
        whole = acc[s, :, HD:]
        some = whole > 0.0
        safe = jnp.where(some, whole, 1.0)
        out[s, 0] = (acc[s, :, :HD] / safe).astype(jnp.bfloat16)
        column = jnp.where(some[:, :1], peak[s] * scale + jnp.log(safe[:, :1]), LOWEST)
        lse[s, 0] = to_row(heads_of(column, group, length), length)


def attend(holds, prefixes, qg, kvg, group):
    slots, heads, rows, _ = qg.shape
    inner, block, _ = kvg.shape
    length = rows // group
    return pl.pallas_call(
        functools.partial(attend_kernel, group),
        grid=(heads,),
        in_specs=[
            pl.BlockSpec(memory_space=pltpu.SMEM),
            pl.BlockSpec(memory_space=pltpu.SMEM),
            pl.BlockSpec((slots, 1, rows, HD), lambda g: (0, g, 0, 0)),
            pl.BlockSpec((inner, block, HD), lambda g: (0, 0, g)),
            pl.BlockSpec((inner, block, HD), lambda g: (0, 0, heads + g)),
        ],
        out_specs=[
            pl.BlockSpec((slots, 1, rows, HD), lambda g: (0, g, 0, 0)),
            pl.BlockSpec((slots, 1, PAD, length), lambda g: (0, g, 0, 0)),
        ],
        scratch_shapes=[
            pltpu.VMEM((inner, block, 2 * HD), jnp.bfloat16),
            pltpu.VMEM((slots, rows, 2 * HD), jnp.float32),
            pltpu.VMEM((slots, rows, 1), jnp.float32),
        ],
        out_shape=[
            jax.ShapeDtypeStruct((slots, heads, rows, HD), jnp.bfloat16),
            jax.ShapeDtypeStruct((slots, heads, PAD, length), jnp.float32),
        ],
        compiler_params=pltpu.CompilerParams(vmem_limit_bytes=48 * MIB),
        name="attend",
    )(holds, prefixes, qg, kvg, kvg)


def finish_kernel(
    cfg, outs, lses, own_out, own_lse, wo,
    result,
    obuf, lbuf, vo, square, context, psend, precv,
    wsem, lsem, osend, orecv, ssend, srecv, xsend, xrecv,
):
    tps, inner, split, slots, kv_heads, group = cfg
    half = kv_heads // split
    length, width = result.shape
    tile = 512 if width % 512 == 0 else width
    req, tp = lax.axis_index("req"), lax.axis_index("tp")
    part = lax.rem(req, split)

    load = pltpu.make_async_copy(wo, vo, wsem.at[0])
    load.start()
    greet(req, tp, slots[1:], range(1, tps))
    short = length // PIECES
    step = group * short
    order = range(len(slots) - 1, 0, -1)
    stats = [
        pltpu.make_async_remote_copy(
            src_ref=lses.at[n],
            dst_ref=lbuf.at[n],
            send_sem=ssend.at[n - 1],
            recv_sem=srecv.at[n - 1],
            device_id=(flip(req, slots[n]), tp),
            device_id_type=MESH,
        )
        for n in order
    ]

    def answer_of(n, piece):
        rows = pl.ds(piece * step, step)
        return pltpu.make_async_remote_copy(
            src_ref=outs.at[n, :, rows],
            dst_ref=obuf.at[n, :, rows],
            send_sem=osend.at[piece, n - 1],
            recv_sem=orecv.at[piece, n - 1],
            device_id=(flip(req, slots[n]), tp),
            device_id_type=MESH,
        )

    answers = [[answer_of(n, piece) for n in order] for piece in range(PIECES)]
    for copy in stats + answers[0]:
        copy.start()
    keeps = [
        pltpu.make_async_copy(outs.at[0], obuf.at[0], lsem.at[0]),
        pltpu.make_async_copy(lses.at[0], lbuf.at[0], lsem.at[1]),
    ]
    for keep in keeps:
        keep.start()
    for copy in keeps + stats:
        copy.wait()

    square[...] = jnp.zeros_like(square)
    terms = OUTER + 1
    for sub in range(split):
        which = flip(part, sub)
        for g in range(half):
            parts = [lbuf[so * split + sub, g] for so in range(OUTER)]
            own = own_lse[which]
            parts.append(own[g * group : (g + 1) * group])
            parts = [p[:group] for p in parts]
            top = functools.reduce(jnp.maximum, parts)
            shares = [jnp.exp(p - top) for p in parts]
            whole = functools.reduce(jnp.add, shares)
            for j, share in enumerate(shares):
                at = ((sub * half + g) * terms + j) * group
                square[at : at + group] = share / whole
    columns = jnp.transpose(square[...])
    def product(target, piece, n):
        at = pl.multiple_of(target * width + n * tile, 128)
        return jnp.dot(
            context[piece * short : (piece + 1) * short],
            vo[:, pl.ds(at, tile)],
            preferred_element_type=jnp.float32,
        ).astype(jnp.bfloat16)

    swaps = []
    for piece in range(PIECES):
        slot_rows = slice(piece * short, (piece + 1) * short)
        if piece + 1 < PIECES:
            for copy, later in zip(answers[piece], answers[piece + 1]):
                copy.wait_send()
                later.start()
            for copy in answers[piece]:
                copy.wait_recv()
        else:
            for copy in answers[piece]:
                copy.wait()
        for sub in range(split):
            which = flip(part, sub)
            for g in range(half):
                for h in range(group):
                    total = jnp.zeros((short, HD), jnp.float32)
                    first = piece * step + h * short
                    rows = slice(first, first + short)
                    for j in range(terms):
                        at = ((sub * half + g) * terms + j) * group + h
                        if j < OUTER:
                            term = obuf[j * split + sub, g, rows]
                        else:
                            term = own_out[which, g, rows]
                        total = total + term.astype(jnp.float32) * columns[slot_rows, at : at + 1]
                    to = pl.multiple_of(((which * half + g) * group + h) * HD, HD)
                    context[slot_rows, pl.ds(to, HD)] = total.astype(jnp.bfloat16)
        if piece == 0:
            load.wait()
        for k in range(1, tps):
            for n in range(width // tile):
                psend[k - 1, slot_rows, n * tile : (n + 1) * tile] = product(
                    flip(tp, k), piece, n
                )
            swap = pltpu.make_async_remote_copy(
                src_ref=psend.at[k - 1, pl.ds(piece * short, short)],
                dst_ref=precv.at[k - 1, pl.ds(piece * short, short)],
                send_sem=xsend.at[piece, k - 1],
                recv_sem=xrecv.at[piece, k - 1],
                device_id=(req, flip(tp, k)),
                device_id_type=MESH,
            )
            swap.start()
            swaps.append((k, slot_rows, swap))
        for n in range(width // tile):
            result[slot_rows, n * tile : (n + 1) * tile] = product(tp, piece, n).astype(
                jnp.float32
            )
    for k, slot_rows, swap in swaps:
        swap.wait()
        result[slot_rows] += precv[k - 1, slot_rows].astype(jnp.float32)


def finish(outs, lses, own_out, own_lse, wo, cfg):
    tps, inner, split, slots, kv_heads, group = cfg
    length = lses.shape[-1]
    width = wo.shape[1] // tps
    vmem = pl.BlockSpec(memory_space=pltpu.VMEM)
    hbm = pl.BlockSpec(memory_space=pl.ANY)
    bf16, f32 = jnp.bfloat16, jnp.float32
    dma = pltpu.SemaphoreType.DMA
    return pl.pallas_call(
        functools.partial(finish_kernel, cfg),
        in_specs=[hbm, hbm, vmem, vmem, hbm],
        out_specs=vmem,
        out_shape=jax.ShapeDtypeStruct((length, width), f32),
        scratch_shapes=[
            pltpu.VMEM(outs.shape, bf16),
            pltpu.VMEM(lses.shape, f32),
            pltpu.VMEM(wo.shape, bf16),
            pltpu.VMEM((128, length), f32),
            pltpu.VMEM((length, wo.shape[0]), bf16),
            pltpu.VMEM((tps - 1, length, width), bf16),
            pltpu.VMEM((tps - 1, length, width), bf16),
            dma((1,)),
            dma((2,)),
            dma((PIECES, len(slots) - 1)),
            dma((PIECES, len(slots) - 1)),
            dma((len(slots) - 1,)),
            dma((len(slots) - 1,)),
            dma((PIECES, tps - 1)),
            dma((PIECES, tps - 1)),
        ],
        compiler_params=pltpu.CompilerParams(
            collective_id=1, has_side_effects=True, vmem_limit_bytes=52 * MIB
        ),
        name="finish",
    )(outs, lses, own_out, own_lse, wo)


def shards(
    hidden_in,
    norm_gain,
    q_weight,
    q_bias,
    k_weight,
    k_bias,
    v_weight,
    v_bias,
    o_weight,
    prefix_kv,
    suffix_len,
    req_prefix,
    block_owner,
):
    length = hidden_in.shape[0]
    devices = lax.axis_size("req")
    tps = lax.axis_size("tp")
    owned = devices // NPREF
    block = prefix_kv.shape[0]
    kv_heads = k_weight.shape[1] // HD
    group = q_weight.shape[1] // k_weight.shape[1]
    inner = devices // OUTER
    split = 2 if kv_heads % 2 == 0 else 1
    slots = tuple(so * inner + sub for so in range(OUTER) for sub in range(split))
    cfg = (tps, inner, split, slots, kv_heads, group)
    me = lax.axis_index("req")

    index = jnp.arange(devices, dtype=jnp.int32)
    blocks = me // inner * inner + (me % inner ^ jnp.arange(inner, dtype=jnp.int32))
    holds = jnp.sum(
        jnp.where(block_owner[None, :] == blocks[:, None], (index // owned)[None, :], 0), axis=1
    )
    prefix = jnp.broadcast_to(req_prefix[:, None], (8, 128))
    kvs = prefix_kv.reshape(block, 2 * kv_heads * HD)
    gain = jnp.broadcast_to(norm_gain.astype(jnp.float32)[None, :], (8, norm_gain.shape[0]))
    bias = jnp.concatenate([q_bias, k_bias, v_bias]).astype(jnp.float32)[None, :]
    cosine, sine = tables(block * owned + np.arange(length))
    qg, kvg, prefixes, own_out, own_lse = project(
        hidden_in, gain, bias, jnp.asarray(cosine), jnp.asarray(sine), prefix, kvs,
        q_weight, k_weight, v_weight, cfg,
    )
    outs, lses = attend(holds, prefixes, qg, kvg, group)
    summed = finish(outs, lses, own_out, own_lse, o_weight, cfg)
    valid = jnp.arange(length, dtype=jnp.int32) < suffix_len[0]
    return jnp.where(valid[:, None], summed, jnp.float32(0.0)).astype(jnp.bfloat16)


def solution(mesh):
    placed = (
        P("req", "tp"),
        P("tp"),
        P(None, "tp"),
        P("tp"),
        P(None, "tp"),
        P("tp"),
        P(None, "tp"),
        P("tp"),
        P("tp", None),
        P("req", None, "tp"),
        P("req"),
        P("req"),
        P(),
    )
    return jax.shard_map(
        shards, mesh=mesh, in_specs=placed, out_specs=P("req", "tp"), check_vma=False
    )
```

```python
import functools

import jax
import jax.numpy as jnp
import numpy as np
from jax import lax
from jax.experimental import pallas as pl
from jax.experimental.pallas import tpu as pltpu
from jax.sharding import PartitionSpec as P

HD = 128
NPREF = 4
OUTER = 4
PIECES = 4
PAD = 8

THETA = 1000000.0
EPSILON = 1e-06
LOWEST = -1e30
MIB = 1024 * 1024
MESH = pl.DeviceIdType.MESH
NT = (((1,), (1,)), ((), ()))


def flip(index, mask):
    bit = 1
    while bit <= mask:
        if mask & bit:
            index = index + bit - 2 * bit * lax.rem(lax.div(index, bit), 2)
        bit *= 2
    return index


def tables(positions):
    freqs = np.float32(THETA) ** (-(np.arange(HD // 2, dtype=np.float32) * 2.0) / HD)
    angles = positions.astype(np.float32)[:, None] * freqs.astype(np.float32)[None, :]
    cosine = np.cos(angles.astype(np.float64)).astype(np.float32)
    sine = np.sin(angles.astype(np.float64)).astype(np.float32)
    return np.concatenate([cosine, cosine], 1), np.concatenate([-sine, sine], 1)


def heads_of(column, group, length):
    short = length // PIECES
    return [
        jnp.concatenate(
            [column[(p * group + h) * short :][:short] for p in range(PIECES)], axis=0
        )
        for h in range(group)
    ]


def greet(req, tp, req_masks, tp_masks):
    barrier = pltpu.get_barrier_semaphore()
    for mask in req_masks:
        pl.semaphore_signal(barrier, inc=1, device_id=(flip(req, mask), tp), device_id_type=MESH)
    for mask in tp_masks:
        pl.semaphore_signal(barrier, inc=1, device_id=(req, flip(tp, mask)), device_id_type=MESH)
    pl.semaphore_wait(barrier, len(req_masks) + len(tp_masks))


def to_row(columns, length):
    lane = lax.broadcasted_iota(jnp.int32, (length, length), 1)
    square = jnp.zeros((length, length), jnp.float32)
    for n, column in enumerate(columns):
        square = jnp.where(lane == n, column, square)
    return jnp.transpose(square)[:PAD]


def project_kernel(
    cfg, hidden, gain, bias, cosine, sine, prefix, kvs, wq, wk, wv,
    qg, kvg, prefixes, own_out, own_lse,
    xbuf, gbuf, normed, vq, vk, vv, qbuf,
    wsem, lsem, xsend, xrecv, gsend, grecv, qsend, qrecv, ksend, krecv, psend, precv,
):
    tps, inner, split, slots, kv_heads, group = cfg
    length, width = hidden.shape
    half = kv_heads // split
    req, tp = lax.axis_index("req"), lax.axis_index("tp")
    part = lax.rem(req, split)
    short = length // PIECES
    span = group * HD
    step = group * short

    def cached(side, which):
        return pl.multiple_of((side * split + which) * half * HD, HD)

    loads = [
        pltpu.make_async_copy(src, dst, wsem.at[n])
        for n, (src, dst) in enumerate(((wq, vq), (wk, vk), (wv, vv)))
    ]
    for load in loads:
        load.start()
    greet(req, tp, sorted(set(slots[1:]) | set(range(1, inner))), range(1, tps))

    def swap_of(k, piece):
        rows = pl.ds(piece * short, short)
        return pltpu.make_async_remote_copy(
            src_ref=hidden.at[rows],
            dst_ref=xbuf.at[tp, rows],
            send_sem=xsend.at[piece, k - 1],
            recv_sem=xrecv.at[piece, k - 1],
            device_id=(req, flip(tp, k)),
            device_id_type=MESH,
        )

    gains = [
        pltpu.make_async_remote_copy(
            src_ref=gain,
            dst_ref=gbuf.at[tp],
            send_sem=gsend.at[k - 1],
            recv_sem=grecv.at[k - 1],
            device_id=(req, flip(tp, k)),
            device_id_type=MESH,
        )
        for k in range(1, tps)
    ]
    for copy in gains:
        copy.start()
    swaps = [[swap_of(k, piece) for k in range(1, tps)] for piece in range(PIECES)]
    for swap in swaps[0]:
        swap.start()
    blocks = []
    for k in range(inner - 1, 0, -1):
        for side in range(2):
            there = lax.rem(flip(req, k), split)
            blocks.append(
                pltpu.make_async_remote_copy(
                    src_ref=kvs.at[:, pl.ds(cached(side, there), half * HD)],
                    dst_ref=kvg.at[k, :, pl.ds(side * half * HD, half * HD)],
                    send_sem=ksend.at[k - 1, side],
                    recv_sem=krecv.at[k - 1, side],
                    device_id=(flip(req, k), tp),
                    device_id_type=MESH,
                )
            )
    for copy in blocks:
        copy.start()
    for n, mask in enumerate(slots[1:]):
        copy = pltpu.make_async_remote_copy(
            src_ref=prefix,
            dst_ref=prefixes.at[n + 1],
            send_sem=psend.at[n],
            recv_sem=precv.at[n],
            device_id=(flip(req, mask), tp),
            device_id_type=MESH,
        )
        copy.start()
        blocks.append(copy)
    keeps = [pltpu.make_async_copy(prefix, prefixes.at[0], lsem.at[0])]
    for side in range(2):
        keeps.append(
            pltpu.make_async_copy(
                kvs.at[:, pl.ds(cached(side, part), half * HD)],
                kvg.at[0, :, pl.ds(side * half * HD, half * HD)],
                lsem.at[1 + side],
            )
        )
    for keep in keeps:
        keep.start()
    xbuf[tp] = hidden[...]
    gbuf[tp] = gain[...]

    def rope(x, at):
        return x * cosine[at] + pltpu.roll(x, HD // 2, 1) * sine[at]

    asks = []
    for piece in range(PIECES):
        at = slice(piece * short, (piece + 1) * short)
        if piece + 1 < PIECES:
            for swap, later in zip(swaps[piece], swaps[piece + 1]):
                swap.wait_send()
                later.start()
                swap.wait_recv()
        else:
            for swap in swaps[piece]:
                swap.wait()
        if piece == 0:
            for copy in gains:
                copy.wait()
        square = jnp.zeros((short, 1), jnp.float32)
        for t in range(tps):
            tokens = xbuf[t, at].astype(jnp.float32)
            square = square + jnp.sum(tokens * tokens, axis=1, keepdims=True)
        factor = lax.rsqrt(square / (tps * width) + EPSILON)
        for t in range(tps):
            tokens = xbuf[t, at].astype(jnp.float32) * factor * gbuf[t][:1]
            normed[at, t * width : (t + 1) * width] = tokens.astype(jnp.bfloat16)
        if piece == 0:
            loads[0].wait()
        for g in range(kv_heads):
            q = jnp.dot(
                normed[at], vq[:, g * span : (g + 1) * span], preferred_element_type=jnp.float32
            )
            q = q + bias[:, g * span : (g + 1) * span]
            for h in range(group):
                to = piece * step + h * short
                qbuf[g // half, g % half, to : to + short] = rope(
                    q[:, h * HD : (h + 1) * HD], at
                ).astype(jnp.bfloat16)
        rows = pl.ds(piece * step, step)
        for n, mask in enumerate(slots[1:]):
            ask = pltpu.make_async_remote_copy(
                src_ref=qbuf.at[lax.rem(flip(req, mask), split), :, rows],
                dst_ref=qg.at[n + 1, :, rows],
                send_sem=qsend.at[piece, n],
                recv_sem=qrecv.at[piece, n],
                device_id=(flip(req, mask), tp),
                device_id_type=MESH,
            )
            ask.start()
            asks.append(ask)
    mine = pltpu.make_async_copy(qbuf.at[part], qg.at[0], lsem.at[3])
    mine.start()
    for load in loads[1:]:
        load.wait()

    first = kv_heads * span
    rows = group * length
    slot = lax.broadcasted_iota(jnp.int32, (rows, length), 0)
    slot = lax.div(slot, step) * short + lax.rem(slot, short)
    allowed = lax.broadcasted_iota(jnp.int32, (rows, length), 1) <= slot
    k_all = jnp.dot(normed[...], vk[...], preferred_element_type=jnp.float32)
    k_all = k_all + bias[:, first : first + kv_heads * HD]
    first += kv_heads * HD
    v_all = jnp.dot(normed[...], vv[...], preferred_element_type=jnp.float32)
    v_all = (v_all + bias[:, first : first + kv_heads * HD]).astype(jnp.bfloat16)
    for p in range(split):
        columns = []
        for g in range(half):
            at = (p * half + g) * HD
            keys = rope(k_all[:, at : at + HD], slice(None)).astype(jnp.bfloat16)
            scores = lax.dot_general(qbuf[p, g], keys, NT, preferred_element_type=jnp.float32)
            scores = jnp.where(allowed, scores * HD ** (-0.5), -jnp.inf)
            top = jnp.max(scores, axis=1, keepdims=True)
            weights = jnp.exp(scores - top)
            total = jnp.sum(weights, axis=1, keepdims=True)
            out = jnp.dot(
                weights.astype(jnp.bfloat16),
                v_all[:, at : at + HD],
                preferred_element_type=jnp.float32,
            )
            own_out[p, g] = (out / total).astype(jnp.bfloat16)
            column = top + jnp.log(total)
            columns += heads_of(column, group, length)
        own_lse[p] = to_row(columns, length)

    for keep in keeps:
        keep.wait()
    mine.wait()
    for copy in asks + blocks:
        copy.wait()


def project(hidden, gain, bias, cosine, sine, prefix, kvs, wq, wk, wv, cfg):
    tps, inner, split, slots, kv_heads, group = cfg
    length, width = hidden.shape
    half = kv_heads // split
    rows = group * length
    vmem = pl.BlockSpec(memory_space=pltpu.VMEM)
    hbm = pl.BlockSpec(memory_space=pl.ANY)
    bf16, f32 = jnp.bfloat16, jnp.float32
    dma = pltpu.SemaphoreType.DMA
    return pl.pallas_call(
        functools.partial(project_kernel, cfg),
        in_specs=[vmem] * 6 + [hbm] * 4,
        out_specs=[hbm, hbm, hbm, vmem, vmem],
        out_shape=[
            jax.ShapeDtypeStruct((len(slots), half, rows, HD), bf16),
            jax.ShapeDtypeStruct((inner, kvs.shape[0], 2 * half * HD), bf16),
            jax.ShapeDtypeStruct((len(slots),) + prefix.shape, jnp.int32),
            jax.ShapeDtypeStruct((split, half, rows, HD), bf16),
            jax.ShapeDtypeStruct((split, PAD, length), f32),
        ],
        scratch_shapes=[
            pltpu.VMEM((tps, length, width), bf16),
            pltpu.VMEM((tps,) + gain.shape, f32),
            pltpu.VMEM((length, tps * width), bf16),
            pltpu.VMEM(wq.shape, bf16),
            pltpu.VMEM(wk.shape, bf16),
            pltpu.VMEM(wv.shape, bf16),
            pltpu.VMEM((split, half, rows, HD), bf16),
            dma((3,)),
            dma((4,)),
            dma((PIECES, tps - 1)),
            dma((PIECES, tps - 1)),
            dma((tps - 1,)),
            dma((tps - 1,)),
            dma((PIECES, len(slots) - 1)),
            dma((PIECES, len(slots) - 1)),
            dma((inner - 1, 2)),
            dma((inner - 1, 2)),
            dma((len(slots) - 1,)),
            dma((len(slots) - 1,)),
        ],
        compiler_params=pltpu.CompilerParams(
            collective_id=0, has_side_effects=True, vmem_limit_bytes=52 * MIB
        ),
        name="project",
    )(hidden, gain, bias, cosine, sine, prefix, kvs, wq, wk, wv)


def attend_kernel(group, holds, prefixes, qs, ks, vs, out, lse, acc, peak, total):
    slots, _, rows, _ = qs.shape
    inner, block, _ = ks.shape
    length = rows // group
    scale = HD ** (-0.5)
    base2 = scale * np.log2(np.e)
    peak[...] = jnp.full_like(peak, LOWEST)
    total[...] = jnp.zeros_like(total)
    acc[...] = jnp.zeros_like(acc)
    part = rows // 2
    halves = [slice(n * part, (n + 1) * part) for n in range(2)]

    @pl.loop(0, slots * inner)
    def _(pair):
        s, k = lax.div(pair, inner), lax.rem(pair, inner)

        @pl.when(prefixes[s, 0, 0] == holds[k])
        def _():
            both = [
                lax.dot_general(qs[s, 0, at], ks[k], NT, preferred_element_type=jnp.float32)
                for at in halves
            ]
            for at, scores in zip(halves, both):
                old = peak[s, at]
                top = jnp.maximum(old, jnp.max(scores, axis=1, keepdims=True))
                weights = jnp.exp2((scores - top) * base2)
                fade = jnp.exp2((old - top) * base2)
                peak[s, at] = top
                total[s, at] = total[s, at] * fade + jnp.sum(weights, axis=1, keepdims=True)
                acc[s, at] = acc[s, at] * fade + jnp.dot(
                    weights.astype(jnp.bfloat16), vs[k], preferred_element_type=jnp.float32
                )

    @pl.loop(0, slots)
    def _(s):
        whole = total[s]
        out[s, 0] = (acc[s] * (1.0 / jnp.where(whole > 0.0, whole, 1.0))).astype(jnp.bfloat16)
        tops = to_row(heads_of(peak[s], group, length), length)
        sums = to_row(heads_of(whole, group, length), length)
        some = sums > 0.0
        lse[s, 0] = jnp.where(some, tops * scale + jnp.log(jnp.where(some, sums, 1.0)), LOWEST)


def attend(holds, prefixes, qg, kvg, group):
    slots, heads, rows, _ = qg.shape
    inner, block, _ = kvg.shape
    length = rows // group
    return pl.pallas_call(
        functools.partial(attend_kernel, group),
        grid=(heads,),
        in_specs=[
            pl.BlockSpec(memory_space=pltpu.SMEM),
            pl.BlockSpec(memory_space=pltpu.SMEM),
            pl.BlockSpec((slots, 1, rows, HD), lambda g: (0, g, 0, 0)),
            pl.BlockSpec((inner, block, HD), lambda g: (0, 0, g)),
            pl.BlockSpec((inner, block, HD), lambda g: (0, 0, heads + g)),
        ],
        out_specs=[
            pl.BlockSpec((slots, 1, rows, HD), lambda g: (0, g, 0, 0)),
            pl.BlockSpec((slots, 1, PAD, length), lambda g: (0, g, 0, 0)),
        ],
        scratch_shapes=[
            pltpu.VMEM((slots, rows, HD), jnp.float32),
            pltpu.VMEM((slots, rows, 1), jnp.float32),
            pltpu.VMEM((slots, rows, 1), jnp.float32),
        ],
        out_shape=[
            jax.ShapeDtypeStruct((slots, heads, rows, HD), jnp.bfloat16),
            jax.ShapeDtypeStruct((slots, heads, PAD, length), jnp.float32),
        ],
        compiler_params=pltpu.CompilerParams(vmem_limit_bytes=60 * MIB),
        name="attend",
    )(holds, prefixes, qg, kvg, kvg)


def finish_kernel(
    cfg, outs, lses, own_out, own_lse, wo,
    result,
    obuf, lbuf, vo, square, context, psend, precv,
    wsem, lsem, osend, orecv, ssend, srecv, xsend, xrecv,
):
    tps, inner, split, slots, kv_heads, group = cfg
    half = kv_heads // split
    length, width = result.shape
    tile = 512 if width % 512 == 0 else width
    req, tp = lax.axis_index("req"), lax.axis_index("tp")
    part = lax.rem(req, split)

    load = pltpu.make_async_copy(wo, vo, wsem.at[0])
    load.start()
    greet(req, tp, slots[1:], range(1, tps))
    short = length // PIECES
    step = group * short
    order = range(len(slots) - 1, 0, -1)
    stats = [
        pltpu.make_async_remote_copy(
            src_ref=lses.at[n],
            dst_ref=lbuf.at[n],
            send_sem=ssend.at[n - 1],
            recv_sem=srecv.at[n - 1],
            device_id=(flip(req, slots[n]), tp),
            device_id_type=MESH,
        )
        for n in order
    ]

    def answer_of(n, piece):
        rows = pl.ds(piece * step, step)
        return pltpu.make_async_remote_copy(
            src_ref=outs.at[n, :, rows],
            dst_ref=obuf.at[n, :, rows],
            send_sem=osend.at[piece, n - 1],
            recv_sem=orecv.at[piece, n - 1],
            device_id=(flip(req, slots[n]), tp),
            device_id_type=MESH,
        )

    answers = [[answer_of(n, piece) for n in order] for piece in range(PIECES)]
    for copy in stats + answers[0]:
        copy.start()
    keeps = [
        pltpu.make_async_copy(outs.at[0], obuf.at[0], lsem.at[0]),
        pltpu.make_async_copy(lses.at[0], lbuf.at[0], lsem.at[1]),
    ]
    for keep in keeps:
        keep.start()
    for copy in keeps + stats:
        copy.wait()

    square[...] = jnp.zeros_like(square)
    terms = OUTER + 1
    for sub in range(split):
        which = flip(part, sub)
        for g in range(half):
            parts = [lbuf[so * split + sub, g] for so in range(OUTER)]
            own = own_lse[which]
            parts.append(own[g * group : (g + 1) * group])
            parts = [p[:group] for p in parts]
            top = functools.reduce(jnp.maximum, parts)
            shares = [jnp.exp(p - top) for p in parts]
            whole = functools.reduce(jnp.add, shares)
            for j, share in enumerate(shares):
                at = ((sub * half + g) * terms + j) * group
                square[at : at + group] = share / whole
    columns = jnp.transpose(square[...])
    def product(target, piece, n):
        at = pl.multiple_of(target * width + n * tile, 128)
        return jnp.dot(
            context[piece * short : (piece + 1) * short],
            vo[:, pl.ds(at, tile)],
            preferred_element_type=jnp.float32,
        ).astype(jnp.bfloat16)

    swaps = []
    for piece in range(PIECES):
        slot_rows = slice(piece * short, (piece + 1) * short)
        if piece + 1 < PIECES:
            for copy, later in zip(answers[piece], answers[piece + 1]):
                copy.wait_send()
                later.start()
            for copy in answers[piece]:
                copy.wait_recv()
        else:
            for copy in answers[piece]:
                copy.wait()
        for sub in range(split):
            which = flip(part, sub)
            for g in range(half):
                for h in range(group):
                    total = jnp.zeros((short, HD), jnp.float32)
                    first = piece * step + h * short
                    rows = slice(first, first + short)
                    for j in range(terms):
                        at = ((sub * half + g) * terms + j) * group + h
                        if j < OUTER:
                            term = obuf[j * split + sub, g, rows]
                        else:
                            term = own_out[which, g, rows]
                        total = total + term.astype(jnp.float32) * columns[slot_rows, at : at + 1]
                    to = pl.multiple_of(((which * half + g) * group + h) * HD, HD)
                    context[slot_rows, pl.ds(to, HD)] = total.astype(jnp.bfloat16)
        if piece == 0:
            load.wait()
        for k in range(1, tps):
            for n in range(width // tile):
                psend[k - 1, slot_rows, n * tile : (n + 1) * tile] = product(
                    flip(tp, k), piece, n
                )
            swap = pltpu.make_async_remote_copy(
                src_ref=psend.at[k - 1, pl.ds(piece * short, short)],
                dst_ref=precv.at[k - 1, pl.ds(piece * short, short)],
                send_sem=xsend.at[piece, k - 1],
                recv_sem=xrecv.at[piece, k - 1],
                device_id=(req, flip(tp, k)),
                device_id_type=MESH,
            )
            swap.start()
            swaps.append((k, slot_rows, swap))
        for n in range(width // tile):
            result[slot_rows, n * tile : (n + 1) * tile] = product(tp, piece, n).astype(
                jnp.float32
            )
    for k, slot_rows, swap in swaps:
        swap.wait()
        result[slot_rows] += precv[k - 1, slot_rows].astype(jnp.float32)


def finish(outs, lses, own_out, own_lse, wo, cfg):
    tps, inner, split, slots, kv_heads, group = cfg
    length = lses.shape[-1]
    width = wo.shape[1] // tps
    vmem = pl.BlockSpec(memory_space=pltpu.VMEM)
    hbm = pl.BlockSpec(memory_space=pl.ANY)
    bf16, f32 = jnp.bfloat16, jnp.float32
    dma = pltpu.SemaphoreType.DMA
    return pl.pallas_call(
        functools.partial(finish_kernel, cfg),
        in_specs=[hbm, hbm, vmem, vmem, hbm],
        out_specs=vmem,
        out_shape=jax.ShapeDtypeStruct((length, width), f32),
        scratch_shapes=[
            pltpu.VMEM(outs.shape, bf16),
            pltpu.VMEM(lses.shape, f32),
            pltpu.VMEM(wo.shape, bf16),
            pltpu.VMEM((128, length), f32),
            pltpu.VMEM((length, wo.shape[0]), bf16),
            pltpu.VMEM((tps - 1, length, width), bf16),
            pltpu.VMEM((tps - 1, length, width), bf16),
            dma((1,)),
            dma((2,)),
            dma((PIECES, len(slots) - 1)),
            dma((PIECES, len(slots) - 1)),
            dma((len(slots) - 1,)),
            dma((len(slots) - 1,)),
            dma((PIECES, tps - 1)),
            dma((PIECES, tps - 1)),
        ],
        compiler_params=pltpu.CompilerParams(
            collective_id=1, has_side_effects=True, vmem_limit_bytes=52 * MIB
        ),
        name="finish",
    )(outs, lses, own_out, own_lse, wo)


def shards(
    hidden_in,
    norm_gain,
    q_weight,
    q_bias,
    k_weight,
    k_bias,
    v_weight,
    v_bias,
    o_weight,
    prefix_kv,
    suffix_len,
    req_prefix,
    block_owner,
):
    length = hidden_in.shape[0]
    devices = lax.axis_size("req")
    tps = lax.axis_size("tp")
    owned = devices // NPREF
    block = prefix_kv.shape[0]
    kv_heads = k_weight.shape[1] // HD
    group = q_weight.shape[1] // k_weight.shape[1]
    inner = devices // OUTER
    split = 2 if kv_heads % 2 == 0 else 1
    slots = tuple(so * inner + sub for so in range(OUTER) for sub in range(split))
    cfg = (tps, inner, split, slots, kv_heads, group)
    me = lax.axis_index("req")

    index = jnp.arange(devices, dtype=jnp.int32)
    blocks = me // inner * inner + (me % inner ^ jnp.arange(inner, dtype=jnp.int32))
    holds = jnp.sum(
        jnp.where(block_owner[None, :] == blocks[:, None], (index // owned)[None, :], 0), axis=1
    )
    prefix = jnp.broadcast_to(req_prefix[:, None], (8, 128))
    kvs = prefix_kv.reshape(block, 2 * kv_heads * HD)
    gain = jnp.broadcast_to(norm_gain.astype(jnp.float32)[None, :], (8, norm_gain.shape[0]))
    bias = jnp.concatenate([q_bias, k_bias, v_bias]).astype(jnp.float32)[None, :]
    cosine, sine = tables(block * owned + np.arange(length))
    qg, kvg, prefixes, own_out, own_lse = project(
        hidden_in, gain, bias, jnp.asarray(cosine), jnp.asarray(sine), prefix, kvs,
        q_weight, k_weight, v_weight, cfg,
    )
    outs, lses = attend(holds, prefixes, qg, kvg, group)
    summed = finish(outs, lses, own_out, own_lse, o_weight, cfg)
    valid = jnp.arange(length, dtype=jnp.int32) < suffix_len[0]
    return jnp.where(valid[:, None], summed, jnp.float32(0.0)).astype(jnp.bfloat16)


def solution(mesh):
    placed = (
        P("req", "tp"),
        P("tp"),
        P(None, "tp"),
        P("tp"),
        P(None, "tp"),
        P("tp"),
        P(None, "tp"),
        P("tp"),
        P("tp", None),
        P("req", None, "tp"),
        P("req"),
        P("req"),
        P(),
    )
    return jax.shard_map(
        shards, mesh=mesh, in_specs=placed, out_specs=P("req", "tp"), check_vma=False
    )
```

```python
import functools

import jax
import jax.numpy as jnp
import numpy as np
from jax import lax
from jax.experimental import pallas as pl
from jax.experimental.pallas import tpu as pltpu
from jax.sharding import PartitionSpec as P

HD = 128
NPREF = 4
OUTER = 4
PIECES = 4
PAD = 8

THETA = 1000000.0
EPSILON = 1e-06
LOWEST = -1e30
MIB = 1024 * 1024
MESH = pl.DeviceIdType.MESH
NT = (((1,), (1,)), ((), ()))


def flip(index, mask):
    bit = 1
    while bit <= mask:
        if mask & bit:
            index = index + bit - 2 * bit * lax.rem(lax.div(index, bit), 2)
        bit *= 2
    return index


def tables(positions):
    freqs = np.float32(THETA) ** (-(np.arange(HD // 2, dtype=np.float32) * 2.0) / HD)
    angles = positions.astype(np.float32)[:, None] * freqs.astype(np.float32)[None, :]
    cosine = np.cos(angles.astype(np.float64)).astype(np.float32)
    sine = np.sin(angles.astype(np.float64)).astype(np.float32)
    return np.concatenate([cosine, cosine], 1), np.concatenate([-sine, sine], 1)


def heads_of(column, group, length):
    short = length // PIECES
    return [
        jnp.concatenate(
            [column[(p * group + h) * short :][:short] for p in range(PIECES)], axis=0
        )
        for h in range(group)
    ]


def greet(req, tp, req_masks, tp_masks):
    barrier = pltpu.get_barrier_semaphore()
    for mask in req_masks:
        pl.semaphore_signal(barrier, inc=1, device_id=(flip(req, mask), tp), device_id_type=MESH)
    for mask in tp_masks:
        pl.semaphore_signal(barrier, inc=1, device_id=(req, flip(tp, mask)), device_id_type=MESH)
    pl.semaphore_wait(barrier, len(req_masks) + len(tp_masks))


def to_row(columns, length):
    lane = lax.broadcasted_iota(jnp.int32, (length, length), 1)
    square = jnp.zeros((length, length), jnp.float32)
    for n, column in enumerate(columns):
        square = jnp.where(lane == n, column, square)
    return jnp.transpose(square)[:PAD]


def project_kernel(
    cfg, hidden, gain, bias, cosine, sine, prefix, kvs, wq, wk, wv,
    qg, kvg, prefixes, own_out, own_lse,
    xbuf, gbuf, normed, vq, vk, vv, qbuf,
    wsem, lsem, xsend, xrecv, gsend, grecv, qsend, qrecv, ksend, krecv, psend, precv,
):
    tps, inner, split, slots, kv_heads, group = cfg
    length, width = hidden.shape
    half = kv_heads // split
    req, tp = lax.axis_index("req"), lax.axis_index("tp")
    part = lax.rem(req, split)
    short = length // PIECES
    span = group * HD
    step = group * short

    def cached(side, which):
        return pl.multiple_of((side * split + which) * half * HD, HD)

    loads = [
        pltpu.make_async_copy(src, dst, wsem.at[n])
        for n, (src, dst) in enumerate(((wq, vq), (wk, vk), (wv, vv)))
    ]
    for load in loads:
        load.start()
    greet(req, tp, sorted(set(slots[1:]) | set(range(1, inner))), range(1, tps))

    def swap_of(k, piece):
        rows = pl.ds(piece * short, short)
        return pltpu.make_async_remote_copy(
            src_ref=hidden.at[rows],
            dst_ref=xbuf.at[tp, rows],
            send_sem=xsend.at[piece, k - 1],
            recv_sem=xrecv.at[piece, k - 1],
            device_id=(req, flip(tp, k)),
            device_id_type=MESH,
        )

    gains = [
        pltpu.make_async_remote_copy(
            src_ref=gain,
            dst_ref=gbuf.at[tp],
            send_sem=gsend.at[k - 1],
            recv_sem=grecv.at[k - 1],
            device_id=(req, flip(tp, k)),
            device_id_type=MESH,
        )
        for k in range(1, tps)
    ]
    for copy in gains:
        copy.start()
    swaps = [[swap_of(k, piece) for k in range(1, tps)] for piece in range(PIECES)]
    for swap in swaps[0]:
        swap.start()
    blocks = []
    for k in range(inner - 1, 0, -1):
        for side in range(2):
            there = lax.rem(flip(req, k), split)
            blocks.append(
                pltpu.make_async_remote_copy(
                    src_ref=kvs.at[:, pl.ds(cached(side, there), half * HD)],
                    dst_ref=kvg.at[k, :, pl.ds(side * half * HD, half * HD)],
                    send_sem=ksend.at[k - 1, side],
                    recv_sem=krecv.at[k - 1, side],
                    device_id=(flip(req, k), tp),
                    device_id_type=MESH,
                )
            )
    for copy in blocks:
        copy.start()
    for n, mask in enumerate(slots[1:]):
        copy = pltpu.make_async_remote_copy(
            src_ref=prefix,
            dst_ref=prefixes.at[n + 1],
            send_sem=psend.at[n],
            recv_sem=precv.at[n],
            device_id=(flip(req, mask), tp),
            device_id_type=MESH,
        )
        copy.start()
        blocks.append(copy)
    keeps = [pltpu.make_async_copy(prefix, prefixes.at[0], lsem.at[0])]
    for side in range(2):
        keeps.append(
            pltpu.make_async_copy(
                kvs.at[:, pl.ds(cached(side, part), half * HD)],
                kvg.at[0, :, pl.ds(side * half * HD, half * HD)],
                lsem.at[1 + side],
            )
        )
    for keep in keeps:
        keep.start()
    xbuf[tp] = hidden[...]
    gbuf[tp] = gain[...]

    def rope(x, at):
        return x * cosine[at] + pltpu.roll(x, HD // 2, 1) * sine[at]

    asks = []
    for piece in range(PIECES):
        at = slice(piece * short, (piece + 1) * short)
        if piece + 1 < PIECES:
            for swap, later in zip(swaps[piece], swaps[piece + 1]):
                swap.wait_send()
                later.start()
                swap.wait_recv()
        else:
            for swap in swaps[piece]:
                swap.wait()
        if piece == 0:
            for copy in gains:
                copy.wait()
        square = jnp.zeros((short, 1), jnp.float32)
        for t in range(tps):
            tokens = xbuf[t, at].astype(jnp.float32)
            square = square + jnp.sum(tokens * tokens, axis=1, keepdims=True)
        factor = lax.rsqrt(square / (tps * width) + EPSILON)
        for t in range(tps):
            tokens = xbuf[t, at].astype(jnp.float32) * factor * gbuf[t][:1]
            normed[at, t * width : (t + 1) * width] = tokens.astype(jnp.bfloat16)
        if piece == 0:
            loads[0].wait()
        for g in range(kv_heads):
            q = jnp.dot(
                normed[at], vq[:, g * span : (g + 1) * span], preferred_element_type=jnp.float32
            )
            q = q + bias[:, g * span : (g + 1) * span]
            for h in range(group):
                to = piece * step + h * short
                qbuf[g // half, g % half, to : to + short] = rope(
                    q[:, h * HD : (h + 1) * HD], at
                ).astype(jnp.bfloat16)
        rows = pl.ds(piece * step, step)
        for n, mask in enumerate(slots[1:]):
            ask = pltpu.make_async_remote_copy(
                src_ref=qbuf.at[lax.rem(flip(req, mask), split), :, rows],
                dst_ref=qg.at[n + 1, :, rows],
                send_sem=qsend.at[piece, n],
                recv_sem=qrecv.at[piece, n],
                device_id=(flip(req, mask), tp),
                device_id_type=MESH,
            )
            ask.start()
            asks.append(ask)
    mine = pltpu.make_async_copy(qbuf.at[part], qg.at[0], lsem.at[3])
    mine.start()
    for load in loads[1:]:
        load.wait()

    first = kv_heads * span
    rows = group * length
    slot = lax.broadcasted_iota(jnp.int32, (rows, length), 0)
    slot = lax.div(slot, step) * short + lax.rem(slot, short)
    allowed = lax.broadcasted_iota(jnp.int32, (rows, length), 1) <= slot
    k_all = jnp.dot(normed[...], vk[...], preferred_element_type=jnp.float32)
    k_all = k_all + bias[:, first : first + kv_heads * HD]
    first += kv_heads * HD
    v_all = jnp.dot(normed[...], vv[...], preferred_element_type=jnp.float32)
    v_all = (v_all + bias[:, first : first + kv_heads * HD]).astype(jnp.bfloat16)
    for p in range(split):
        columns = []
        for g in range(half):
            at = (p * half + g) * HD
            keys = rope(k_all[:, at : at + HD], slice(None)).astype(jnp.bfloat16)
            scores = lax.dot_general(qbuf[p, g], keys, NT, preferred_element_type=jnp.float32)
            scores = jnp.where(allowed, scores * HD ** (-0.5), -jnp.inf)
            top = jnp.max(scores, axis=1, keepdims=True)
            weights = jnp.exp(scores - top)
            total = jnp.sum(weights, axis=1, keepdims=True)
            out = jnp.dot(
                weights.astype(jnp.bfloat16),
                v_all[:, at : at + HD],
                preferred_element_type=jnp.float32,
            )
            own_out[p, g] = (out / total).astype(jnp.bfloat16)
            column = top + jnp.log(total)
            columns += heads_of(column, group, length)
        own_lse[p] = to_row(columns, length)

    for keep in keeps:
        keep.wait()
    mine.wait()
    for copy in asks + blocks:
        copy.wait()


def project(hidden, gain, bias, cosine, sine, prefix, kvs, wq, wk, wv, cfg):
    tps, inner, split, slots, kv_heads, group = cfg
    length, width = hidden.shape
    half = kv_heads // split
    rows = group * length
    vmem = pl.BlockSpec(memory_space=pltpu.VMEM)
    hbm = pl.BlockSpec(memory_space=pl.ANY)
    bf16, f32 = jnp.bfloat16, jnp.float32
    dma = pltpu.SemaphoreType.DMA
    return pl.pallas_call(
        functools.partial(project_kernel, cfg),
        in_specs=[vmem] * 6 + [hbm] * 4,
        out_specs=[hbm, hbm, hbm, vmem, vmem],
        out_shape=[
            jax.ShapeDtypeStruct((len(slots), half, rows, HD), bf16),
            jax.ShapeDtypeStruct((inner, kvs.shape[0], 2 * half * HD), bf16),
            jax.ShapeDtypeStruct((len(slots),) + prefix.shape, jnp.int32),
            jax.ShapeDtypeStruct((split, half, rows, HD), bf16),
            jax.ShapeDtypeStruct((split, PAD, length), f32),
        ],
        scratch_shapes=[
            pltpu.VMEM((tps, length, width), bf16),
            pltpu.VMEM((tps,) + gain.shape, f32),
            pltpu.VMEM((length, tps * width), bf16),
            pltpu.VMEM(wq.shape, bf16),
            pltpu.VMEM(wk.shape, bf16),
            pltpu.VMEM(wv.shape, bf16),
            pltpu.VMEM((split, half, rows, HD), bf16),
            dma((3,)),
            dma((4,)),
            dma((PIECES, tps - 1)),
            dma((PIECES, tps - 1)),
            dma((tps - 1,)),
            dma((tps - 1,)),
            dma((PIECES, len(slots) - 1)),
            dma((PIECES, len(slots) - 1)),
            dma((inner - 1, 2)),
            dma((inner - 1, 2)),
            dma((len(slots) - 1,)),
            dma((len(slots) - 1,)),
        ],
        compiler_params=pltpu.CompilerParams(
            collective_id=0, has_side_effects=True, vmem_limit_bytes=52 * MIB
        ),
        name="project",
    )(hidden, gain, bias, cosine, sine, prefix, kvs, wq, wk, wv)


def attend_kernel(group, owners, facts, qs, ks, vs, out, lse, acc, peak, total, holds):
    slots, _, rows, _ = qs.shape
    inner, block, _ = ks.shape
    devices = owners.shape[0]
    owned = devices // NPREF
    length = rows // group
    short = length // PIECES
    step = group * short
    scale = HD ** (-0.5)
    base2 = scale * np.log2(np.e)
    peak[...] = jnp.full_like(peak, LOWEST)
    total[...] = jnp.zeros_like(total)
    acc[...] = jnp.zeros_like(acc)

    me = lax.axis_index("req")
    for k in range(inner):
        there = flip(me, k)
        prefix = jnp.int32(0)
        for j in range(devices):
            prefix = jnp.where(owners[j] == there, jnp.int32(j // owned), prefix)
        holds[k] = prefix

    def update(s, k, count):
        cut = (count // 2) * step
        parts = [slice(a, b) for a, b in ((0, cut), (cut, count * step)) if b > a]
        both = [
            lax.dot_general(qs[s, 0, at], ks[k], NT, preferred_element_type=jnp.float32)
            for at in parts
        ]
        for at, scores in zip(parts, both):
            old = peak[s, at]
            top = jnp.maximum(old, jnp.max(scores, axis=1, keepdims=True))
            weights = jnp.exp2((scores - top) * base2)
            fade = jnp.exp2((old - top) * base2)
            peak[s, at] = top
            total[s, at] = total[s, at] * fade + jnp.sum(weights, axis=1, keepdims=True)
            acc[s, at] = acc[s, at] * fade + jnp.dot(
                weights.astype(jnp.bfloat16), vs[k], preferred_element_type=jnp.float32
            )

    @pl.loop(0, slots * inner)
    def _(pair):
        s, k = lax.div(pair, inner), lax.rem(pair, inner)

        @pl.when(facts[s, 0, 0] == holds[k])
        def _():
            count = lax.div(facts[s, 1, 0] + (short - 1), short)
            for pieces in range(1, PIECES + 1):
                pl.when(count == pieces)(functools.partial(update, s, k, pieces))

    lane = lax.broadcasted_iota(jnp.int32, (length, 128), 1)
    square = jnp.zeros((length, 128), jnp.float32)
    for s in range(slots):
        whole = total[s]
        out[s, 0] = (acc[s] * (1.0 / jnp.where(whole > 0.0, whole, 1.0))).astype(jnp.bfloat16)
        for first, columns in ((0, peak[s]), (slots * PAD, whole)):
            for h, column in enumerate(heads_of(columns, group, length)):
                square = jnp.where(lane == first + s * PAD + h, column, square)
    square = jnp.transpose(square)
    tops, sums = square[: slots * PAD], square[slots * PAD : 2 * slots * PAD]
    some = sums > 0.0
    result = jnp.where(some, tops * scale + jnp.log(jnp.where(some, sums, 1.0)), LOWEST)
    for s in range(slots):
        lse[s, 0] = result[s * PAD : (s + 1) * PAD]


def attend(owners, facts, qg, kvg, group):
    slots, heads, rows, _ = qg.shape
    inner, block, _ = kvg.shape
    length = rows // group
    return pl.pallas_call(
        functools.partial(attend_kernel, group),
        grid=(heads,),
        in_specs=[
            pl.BlockSpec(memory_space=pltpu.SMEM),
            pl.BlockSpec(memory_space=pltpu.SMEM),
            pl.BlockSpec((slots, 1, rows, HD), lambda g: (0, g, 0, 0)),
            pl.BlockSpec((inner, block, HD), lambda g: (0, 0, g)),
            pl.BlockSpec((inner, block, HD), lambda g: (0, 0, heads + g)),
        ],
        out_specs=[
            pl.BlockSpec((slots, 1, rows, HD), lambda g: (0, g, 0, 0)),
            pl.BlockSpec((slots, 1, PAD, length), lambda g: (0, g, 0, 0)),
        ],
        scratch_shapes=[
            pltpu.VMEM((slots, rows, HD), jnp.float32),
            pltpu.VMEM((slots, rows, 1), jnp.float32),
            pltpu.VMEM((slots, rows, 1), jnp.float32),
            pltpu.SMEM((inner,), jnp.int32),
        ],
        out_shape=[
            jax.ShapeDtypeStruct((slots, heads, rows, HD), jnp.bfloat16),
            jax.ShapeDtypeStruct((slots, heads, PAD, length), jnp.float32),
        ],
        compiler_params=pltpu.CompilerParams(vmem_limit_bytes=60 * MIB),
        name="attend",
    )(owners, facts, qg, kvg, kvg)


def finish_kernel(
    cfg, outs, lses, own_out, own_lse, wo,
    result,
    obuf, lbuf, vo, square, context, psend, precv,
    wsem, lsem, osend, orecv, ssend, srecv, xsend, xrecv,
):
    tps, inner, split, slots, kv_heads, group = cfg
    half = kv_heads // split
    length, width = result.shape
    tile = 512 if width % 512 == 0 else width
    req, tp = lax.axis_index("req"), lax.axis_index("tp")
    part = lax.rem(req, split)

    load = pltpu.make_async_copy(wo, vo, wsem.at[0])
    load.start()
    greet(req, tp, slots[1:], range(1, tps))
    short = length // PIECES
    step = group * short
    order = range(len(slots) - 1, 0, -1)
    stats = [
        pltpu.make_async_remote_copy(
            src_ref=lses.at[n],
            dst_ref=lbuf.at[n],
            send_sem=ssend.at[n - 1],
            recv_sem=srecv.at[n - 1],
            device_id=(flip(req, slots[n]), tp),
            device_id_type=MESH,
        )
        for n in order
    ]

    def answer_of(n, piece):
        rows = pl.ds(piece * step, step)
        return pltpu.make_async_remote_copy(
            src_ref=outs.at[n, :, rows],
            dst_ref=obuf.at[n, :, rows],
            send_sem=osend.at[piece, n - 1],
            recv_sem=orecv.at[piece, n - 1],
            device_id=(flip(req, slots[n]), tp),
            device_id_type=MESH,
        )

    answers = [[answer_of(n, piece) for n in order] for piece in range(PIECES)]
    for copy in stats + answers[0]:
        copy.start()
    keeps = [
        pltpu.make_async_copy(outs.at[0], obuf.at[0], lsem.at[0]),
        pltpu.make_async_copy(lses.at[0], lbuf.at[0], lsem.at[1]),
    ]
    for keep in keeps:
        keep.start()
    for copy in keeps + stats:
        copy.wait()

    square[...] = jnp.zeros_like(square)
    terms = OUTER + 1
    for sub in range(split):
        which = flip(part, sub)
        for g in range(half):
            parts = [lbuf[so * split + sub, g] for so in range(OUTER)]
            own = own_lse[which]
            parts.append(own[g * group : (g + 1) * group])
            parts = [p[:group] for p in parts]
            top = functools.reduce(jnp.maximum, parts)
            shares = [jnp.exp(p - top) for p in parts]
            whole = functools.reduce(jnp.add, shares)
            for j, share in enumerate(shares):
                at = ((sub * half + g) * terms + j) * group
                square[at : at + group] = share / whole
    columns = jnp.transpose(square[...])
    def product(target, piece, n):
        at = pl.multiple_of(target * width + n * tile, 128)
        return jnp.dot(
            context[piece * short : (piece + 1) * short],
            vo[:, pl.ds(at, tile)],
            preferred_element_type=jnp.float32,
        ).astype(jnp.bfloat16)

    swaps = []
    for piece in range(PIECES):
        slot_rows = slice(piece * short, (piece + 1) * short)
        if piece + 1 < PIECES:
            for copy, later in zip(answers[piece], answers[piece + 1]):
                copy.wait_send()
                later.start()
            for copy in answers[piece]:
                copy.wait_recv()
        else:
            for copy in answers[piece]:
                copy.wait()
        for sub in range(split):
            which = flip(part, sub)
            for g in range(half):
                for h in range(group):
                    total = jnp.zeros((short, HD), jnp.float32)
                    first = piece * step + h * short
                    rows = slice(first, first + short)
                    for j in range(terms):
                        at = ((sub * half + g) * terms + j) * group + h
                        if j < OUTER:
                            term = obuf[j * split + sub, g, rows]
                        else:
                            term = own_out[which, g, rows]
                        total = total + term.astype(jnp.float32) * columns[slot_rows, at : at + 1]
                    to = pl.multiple_of(((which * half + g) * group + h) * HD, HD)
                    context[slot_rows, pl.ds(to, HD)] = total.astype(jnp.bfloat16)
        if piece == 0:
            load.wait()
        for k in range(1, tps):
            for n in range(width // tile):
                psend[k - 1, slot_rows, n * tile : (n + 1) * tile] = product(
                    flip(tp, k), piece, n
                )
            swap = pltpu.make_async_remote_copy(
                src_ref=psend.at[k - 1, pl.ds(piece * short, short)],
                dst_ref=precv.at[k - 1, pl.ds(piece * short, short)],
                send_sem=xsend.at[piece, k - 1],
                recv_sem=xrecv.at[piece, k - 1],
                device_id=(req, flip(tp, k)),
                device_id_type=MESH,
            )
            swap.start()
            swaps.append((k, slot_rows, swap))
        for n in range(width // tile):
            result[slot_rows, n * tile : (n + 1) * tile] = product(tp, piece, n).astype(
                jnp.float32
            )
    for k, slot_rows, swap in swaps:
        swap.wait()
        result[slot_rows] += precv[k - 1, slot_rows].astype(jnp.float32)


def finish(outs, lses, own_out, own_lse, wo, cfg):
    tps, inner, split, slots, kv_heads, group = cfg
    length = lses.shape[-1]
    width = wo.shape[1] // tps
    vmem = pl.BlockSpec(memory_space=pltpu.VMEM)
    hbm = pl.BlockSpec(memory_space=pl.ANY)
    bf16, f32 = jnp.bfloat16, jnp.float32
    dma = pltpu.SemaphoreType.DMA
    return pl.pallas_call(
        functools.partial(finish_kernel, cfg),
        in_specs=[hbm, hbm, vmem, vmem, hbm],
        out_specs=vmem,
        out_shape=jax.ShapeDtypeStruct((length, width), f32),
        scratch_shapes=[
            pltpu.VMEM(outs.shape, bf16),
            pltpu.VMEM(lses.shape, f32),
            pltpu.VMEM(wo.shape, bf16),
            pltpu.VMEM((128, length), f32),
            pltpu.VMEM((length, wo.shape[0]), bf16),
            pltpu.VMEM((tps - 1, length, width), bf16),
            pltpu.VMEM((tps - 1, length, width), bf16),
            dma((1,)),
            dma((2,)),
            dma((PIECES, len(slots) - 1)),
            dma((PIECES, len(slots) - 1)),
            dma((len(slots) - 1,)),
            dma((len(slots) - 1,)),
            dma((PIECES, tps - 1)),
            dma((PIECES, tps - 1)),
        ],
        compiler_params=pltpu.CompilerParams(
            collective_id=1, has_side_effects=True, vmem_limit_bytes=52 * MIB
        ),
        name="finish",
    )(outs, lses, own_out, own_lse, wo)


def shards(
    hidden_in,
    norm_gain,
    q_weight,
    q_bias,
    k_weight,
    k_bias,
    v_weight,
    v_bias,
    o_weight,
    prefix_kv,
    suffix_len,
    req_prefix,
    block_owner,
):
    length = hidden_in.shape[0]
    devices = lax.axis_size("req")
    tps = lax.axis_size("tp")
    owned = devices // NPREF
    block = prefix_kv.shape[0]
    kv_heads = k_weight.shape[1] // HD
    group = q_weight.shape[1] // k_weight.shape[1]
    inner = devices // OUTER
    split = 2 if kv_heads % 2 == 0 else 1
    slots = tuple(so * inner + sub for so in range(OUTER) for sub in range(split))
    cfg = (tps, inner, split, slots, kv_heads, group)

    facts = jnp.concatenate([req_prefix, jnp.broadcast_to(suffix_len, (7,))])
    facts = jnp.broadcast_to(facts[:, None], (8, 128))
    kvs = prefix_kv.reshape(block, 2 * kv_heads * HD)
    gain = jnp.broadcast_to(norm_gain.astype(jnp.float32)[None, :], (8, norm_gain.shape[0]))
    bias = jnp.concatenate([q_bias, k_bias, v_bias]).astype(jnp.float32)[None, :]
    cosine, sine = tables(block * owned + np.arange(length))
    qg, kvg, facts, own_out, own_lse = project(
        hidden_in, gain, bias, jnp.asarray(cosine), jnp.asarray(sine), facts, kvs,
        q_weight, k_weight, v_weight, cfg,
    )
    outs, lses = attend(block_owner, facts, qg, kvg, group)
    summed = finish(outs, lses, own_out, own_lse, o_weight, cfg)
    valid = jnp.arange(length, dtype=jnp.int32) < suffix_len[0]
    return jnp.where(valid[:, None], summed, jnp.float32(0.0)).astype(jnp.bfloat16)


def solution(mesh):
    placed = (
        P("req", "tp"),
        P("tp"),
        P(None, "tp"),
        P("tp"),
        P(None, "tp"),
        P("tp"),
        P(None, "tp"),
        P("tp"),
        P("tp", None),
        P("req", None, "tp"),
        P("req"),
        P("req"),
        P(),
    )
    return jax.shard_map(
        shards, mesh=mesh, in_specs=placed, out_specs=P("req", "tp"), check_vma=False
    )
```

```python
import functools

import jax
import jax.numpy as jnp
import numpy as np
from jax import lax
from jax.experimental import pallas as pl
from jax.experimental.pallas import tpu as pltpu
from jax.sharding import PartitionSpec as P

HD = 128
NPREF = 4
OUTER = 4
PIECES = 4
PAD = 8

THETA = 1000000.0
EPSILON = 1e-06
LOWEST = -1e30
MIB = 1024 * 1024
MESH = pl.DeviceIdType.MESH
NT = (((1,), (1,)), ((), ()))


def flip(index, mask):
    bit = 1
    while bit <= mask:
        if mask & bit:
            index = index + bit - 2 * bit * lax.rem(lax.div(index, bit), 2)
        bit *= 2
    return index


def tables(positions):
    freqs = np.float32(THETA) ** (-(np.arange(HD // 2, dtype=np.float32) * 2.0) / HD)
    angles = positions.astype(np.float32)[:, None] * freqs.astype(np.float32)[None, :]
    cosine = np.cos(angles.astype(np.float64)).astype(np.float32)
    sine = np.sin(angles.astype(np.float64)).astype(np.float32)
    return np.concatenate([cosine, cosine], 1), np.concatenate([-sine, sine], 1)


def heads_of(column, group, length):
    short = length // PIECES
    return [
        jnp.concatenate(
            [column[(p * group + h) * short :][:short] for p in range(PIECES)], axis=0
        )
        for h in range(group)
    ]


def greet(req, tp, req_masks, tp_masks):
    barrier = pltpu.get_barrier_semaphore()
    for mask in req_masks:
        pl.semaphore_signal(barrier, inc=1, device_id=(flip(req, mask), tp), device_id_type=MESH)
    for mask in tp_masks:
        pl.semaphore_signal(barrier, inc=1, device_id=(req, flip(tp, mask)), device_id_type=MESH)
    pl.semaphore_wait(barrier, len(req_masks) + len(tp_masks))


def to_row(columns, length):
    lane = lax.broadcasted_iota(jnp.int32, (length, length), 1)
    square = jnp.zeros((length, length), jnp.float32)
    for n, column in enumerate(columns):
        square = jnp.where(lane == n, column, square)
    return jnp.transpose(square)[:PAD]


def project_kernel(
    cfg, hidden, params, cosine, sine, prefix, kvs, wq, wk, wv,
    qg, kvg, prefixes, own_out, own_lse,
    xbuf, gbuf, normed, vq, vk, vv, qbuf,
    wsem, lsem, xsend, xrecv, gsend, grecv, qsend, qrecv, ksend, krecv, psend, precv,
):
    tps, inner, split, slots, kv_heads, group = cfg
    length, width = hidden.shape
    half = kv_heads // split
    req, tp = lax.axis_index("req"), lax.axis_index("tp")
    part = lax.rem(req, split)
    short = length // PIECES
    span = group * HD
    step = group * short

    def cached(side, which):
        return pl.multiple_of((side * split + which) * half * HD, HD)

    loads = [
        pltpu.make_async_copy(src, dst, wsem.at[n])
        for n, (src, dst) in enumerate(((wq, vq), (wk, vk), (wv, vv)))
    ]
    for load in loads:
        load.start()
    greet(req, tp, sorted(set(slots[1:]) | set(range(1, inner))), range(1, tps))

    def swap_of(k, piece):
        rows = pl.ds(piece * short, short)
        return pltpu.make_async_remote_copy(
            src_ref=hidden.at[rows],
            dst_ref=xbuf.at[tp, rows],
            send_sem=xsend.at[piece, k - 1],
            recv_sem=xrecv.at[piece, k - 1],
            device_id=(req, flip(tp, k)),
            device_id_type=MESH,
        )

    gains = [
        pltpu.make_async_remote_copy(
            src_ref=params.at[:, pl.ds(0, width)],
            dst_ref=gbuf.at[tp],
            send_sem=gsend.at[k - 1],
            recv_sem=grecv.at[k - 1],
            device_id=(req, flip(tp, k)),
            device_id_type=MESH,
        )
        for k in range(1, tps)
    ]
    for copy in gains:
        copy.start()
    swaps = [[swap_of(k, piece) for k in range(1, tps)] for piece in range(PIECES)]
    for swap in swaps[0]:
        swap.start()
    blocks = []
    for k in range(inner - 1, 0, -1):
        for side in range(2):
            there = lax.rem(flip(req, k), split)
            blocks.append(
                pltpu.make_async_remote_copy(
                    src_ref=kvs.at[:, pl.ds(cached(side, there), half * HD)],
                    dst_ref=kvg.at[k, :, pl.ds(side * half * HD, half * HD)],
                    send_sem=ksend.at[k - 1, side],
                    recv_sem=krecv.at[k - 1, side],
                    device_id=(flip(req, k), tp),
                    device_id_type=MESH,
                )
            )
    for copy in blocks:
        copy.start()
    for n, mask in enumerate(slots[1:]):
        copy = pltpu.make_async_remote_copy(
            src_ref=prefix,
            dst_ref=prefixes.at[n + 1],
            send_sem=psend.at[n],
            recv_sem=precv.at[n],
            device_id=(flip(req, mask), tp),
            device_id_type=MESH,
        )
        copy.start()
        blocks.append(copy)
    keeps = [pltpu.make_async_copy(prefix, prefixes.at[0], lsem.at[0])]
    for side in range(2):
        keeps.append(
            pltpu.make_async_copy(
                kvs.at[:, pl.ds(cached(side, part), half * HD)],
                kvg.at[0, :, pl.ds(side * half * HD, half * HD)],
                lsem.at[1 + side],
            )
        )
    for keep in keeps:
        keep.start()
    xbuf[tp] = hidden[...]
    gbuf[tp] = params[:, :width]

    def rope(x, at):
        return x * cosine[at] + pltpu.roll(x, HD // 2, 1) * sine[at]

    asks = []
    for piece in range(PIECES):
        at = slice(piece * short, (piece + 1) * short)
        if piece + 1 < PIECES:
            for swap, later in zip(swaps[piece], swaps[piece + 1]):
                swap.wait_send()
                later.start()
                swap.wait_recv()
        else:
            for swap in swaps[piece]:
                swap.wait()
        if piece == 0:
            for copy in gains:
                copy.wait()
        square = jnp.zeros((short, 1), jnp.float32)
        for t in range(tps):
            tokens = xbuf[t, at].astype(jnp.float32)
            square = square + jnp.sum(tokens * tokens, axis=1, keepdims=True)
        factor = lax.rsqrt(square / (tps * width) + EPSILON)
        for t in range(tps):
            tokens = xbuf[t, at].astype(jnp.float32) * factor * gbuf[t][:1]
            normed[at, t * width : (t + 1) * width] = tokens.astype(jnp.bfloat16)
        if piece == 0:
            loads[0].wait()
        for g in range(kv_heads):
            q = jnp.dot(
                normed[at], vq[:, g * span : (g + 1) * span], preferred_element_type=jnp.float32
            )
            q = q + params[:1, width + g * span : width + (g + 1) * span]
            for h in range(group):
                to = piece * step + h * short
                qbuf[g // half, g % half, to : to + short] = rope(
                    q[:, h * HD : (h + 1) * HD], at
                ).astype(jnp.bfloat16)
        rows = pl.ds(piece * step, step)
        for n, mask in enumerate(slots[1:]):
            ask = pltpu.make_async_remote_copy(
                src_ref=qbuf.at[lax.rem(flip(req, mask), split), :, rows],
                dst_ref=qg.at[n + 1, :, rows],
                send_sem=qsend.at[piece, n],
                recv_sem=qrecv.at[piece, n],
                device_id=(flip(req, mask), tp),
                device_id_type=MESH,
            )
            ask.start()
            asks.append(ask)
    mine = pltpu.make_async_copy(qbuf.at[part], qg.at[0], lsem.at[3])
    mine.start()
    for load in loads[1:]:
        load.wait()

    first = width + kv_heads * span
    rows = group * length
    slot = lax.broadcasted_iota(jnp.int32, (rows, length), 0)
    slot = lax.div(slot, step) * short + lax.rem(slot, short)
    allowed = lax.broadcasted_iota(jnp.int32, (rows, length), 1) <= slot
    k_all = jnp.dot(normed[...], vk[...], preferred_element_type=jnp.float32)
    k_all = k_all + params[:1, first : first + kv_heads * HD]
    first += kv_heads * HD
    v_all = jnp.dot(normed[...], vv[...], preferred_element_type=jnp.float32)
    v_all = (v_all + params[:1, first : first + kv_heads * HD]).astype(jnp.bfloat16)
    for p in range(split):
        columns = []
        for g in range(half):
            at = (p * half + g) * HD
            keys = rope(k_all[:, at : at + HD], slice(None)).astype(jnp.bfloat16)
            scores = lax.dot_general(qbuf[p, g], keys, NT, preferred_element_type=jnp.float32)
            scores = jnp.where(allowed, scores * HD ** (-0.5), -jnp.inf)
            top = jnp.max(scores, axis=1, keepdims=True)
            weights = jnp.exp(scores - top)
            total = jnp.sum(weights, axis=1, keepdims=True)
            out = jnp.dot(
                weights.astype(jnp.bfloat16),
                v_all[:, at : at + HD],
                preferred_element_type=jnp.float32,
            )
            own_out[p, g] = (out / total).astype(jnp.bfloat16)
            column = top + jnp.log(total)
            columns += heads_of(column, group, length)
        own_lse[p] = to_row(columns, length)

    for keep in keeps:
        keep.wait()
    mine.wait()
    for copy in asks + blocks:
        copy.wait()


def project(hidden, params, cosine, sine, prefix, kvs, wq, wk, wv, cfg):
    tps, inner, split, slots, kv_heads, group = cfg
    length, width = hidden.shape
    half = kv_heads // split
    rows = group * length
    vmem = pl.BlockSpec(memory_space=pltpu.VMEM)
    hbm = pl.BlockSpec(memory_space=pl.ANY)
    bf16, f32 = jnp.bfloat16, jnp.float32
    dma = pltpu.SemaphoreType.DMA
    return pl.pallas_call(
        functools.partial(project_kernel, cfg),
        in_specs=[vmem] * 5 + [hbm] * 4,
        out_specs=[hbm, hbm, hbm, vmem, vmem],
        out_shape=[
            jax.ShapeDtypeStruct((len(slots), half, rows, HD), bf16),
            jax.ShapeDtypeStruct((inner, kvs.shape[0], 2 * half * HD), bf16),
            jax.ShapeDtypeStruct((len(slots),) + prefix.shape, jnp.int32),
            jax.ShapeDtypeStruct((split, half, rows, HD), bf16),
            jax.ShapeDtypeStruct((split, PAD, length), f32),
        ],
        scratch_shapes=[
            pltpu.VMEM((tps, length, width), bf16),
            pltpu.VMEM((tps, 8, width), f32),
            pltpu.VMEM((length, tps * width), bf16),
            pltpu.VMEM(wq.shape, bf16),
            pltpu.VMEM(wk.shape, bf16),
            pltpu.VMEM(wv.shape, bf16),
            pltpu.VMEM((split, half, rows, HD), bf16),
            dma((3,)),
            dma((4,)),
            dma((PIECES, tps - 1)),
            dma((PIECES, tps - 1)),
            dma((tps - 1,)),
            dma((tps - 1,)),
            dma((PIECES, len(slots) - 1)),
            dma((PIECES, len(slots) - 1)),
            dma((inner - 1, 2)),
            dma((inner - 1, 2)),
            dma((len(slots) - 1,)),
            dma((len(slots) - 1,)),
        ],
        compiler_params=pltpu.CompilerParams(
            collective_id=0, has_side_effects=True, vmem_limit_bytes=52 * MIB
        ),
        name="project",
    )(hidden, params, cosine, sine, prefix, kvs, wq, wk, wv)


def attend_kernel(group, owners, facts, qs, ks, vs, out, lse, acc, peak, total, holds):
    slots, _, rows, _ = qs.shape
    inner, block, _ = ks.shape
    devices = owners.shape[0]
    owned = devices // NPREF
    length = rows // group
    short = length // PIECES
    step = group * short
    scale = HD ** (-0.5)
    base2 = scale * np.log2(np.e)
    peak[...] = jnp.full_like(peak, LOWEST)
    total[...] = jnp.zeros_like(total)
    acc[...] = jnp.zeros_like(acc)

    me = lax.axis_index("req")
    for k in range(inner):
        there = flip(me, k)
        prefix = jnp.int32(0)
        for j in range(devices):
            prefix = jnp.where(owners[j] == there, jnp.int32(j // owned), prefix)
        holds[k] = prefix

    def update(s, k, count):
        cut = (count // 2) * step
        parts = [slice(a, b) for a, b in ((0, cut), (cut, count * step)) if b > a]
        both = [
            lax.dot_general(qs[s, 0, at], ks[k], NT, preferred_element_type=jnp.float32)
            for at in parts
        ]
        for at, scores in zip(parts, both):
            old = peak[s, at]
            top = jnp.maximum(old, jnp.max(scores, axis=1, keepdims=True))
            weights = jnp.exp2((scores - top) * base2)
            fade = jnp.exp2((old - top) * base2)
            peak[s, at] = top
            total[s, at] = total[s, at] * fade + jnp.sum(weights, axis=1, keepdims=True)
            acc[s, at] = acc[s, at] * fade + jnp.dot(
                weights.astype(jnp.bfloat16), vs[k], preferred_element_type=jnp.float32
            )

    @pl.loop(0, slots * inner)
    def _(pair):
        s, k = lax.div(pair, inner), lax.rem(pair, inner)

        @pl.when(facts[s, 0, 0] == holds[k])
        def _():
            count = lax.div(facts[s, 1, 0] + (short - 1), short)
            for pieces in range(1, PIECES + 1):
                pl.when(count == pieces)(functools.partial(update, s, k, pieces))

    lane = lax.broadcasted_iota(jnp.int32, (length, 128), 1)
    square = jnp.zeros((length, 128), jnp.float32)
    for s in range(slots):
        whole = total[s]
        out[s, 0] = (acc[s] * (1.0 / jnp.where(whole > 0.0, whole, 1.0))).astype(jnp.bfloat16)
        for first, columns in ((0, peak[s]), (slots * PAD, whole)):
            for h, column in enumerate(heads_of(columns, group, length)):
                square = jnp.where(lane == first + s * PAD + h, column, square)
    square = jnp.transpose(square)
    tops, sums = square[: slots * PAD], square[slots * PAD : 2 * slots * PAD]
    some = sums > 0.0
    result = jnp.where(some, tops * scale + jnp.log(jnp.where(some, sums, 1.0)), LOWEST)
    for s in range(slots):
        lse[s, 0] = result[s * PAD : (s + 1) * PAD]


def attend(owners, facts, qg, kvg, group):
    slots, heads, rows, _ = qg.shape
    inner, block, _ = kvg.shape
    length = rows // group
    return pl.pallas_call(
        functools.partial(attend_kernel, group),
        grid=(heads,),
        in_specs=[
            pl.BlockSpec(memory_space=pltpu.SMEM),
            pl.BlockSpec(memory_space=pltpu.SMEM),
            pl.BlockSpec((slots, 1, rows, HD), lambda g: (0, g, 0, 0)),
            pl.BlockSpec((inner, block, HD), lambda g: (0, 0, g)),
            pl.BlockSpec((inner, block, HD), lambda g: (0, 0, heads + g)),
        ],
        out_specs=[
            pl.BlockSpec((slots, 1, rows, HD), lambda g: (0, g, 0, 0)),
            pl.BlockSpec((slots, 1, PAD, length), lambda g: (0, g, 0, 0)),
        ],
        scratch_shapes=[
            pltpu.VMEM((slots, rows, HD), jnp.float32),
            pltpu.VMEM((slots, rows, 1), jnp.float32),
            pltpu.VMEM((slots, rows, 1), jnp.float32),
            pltpu.SMEM((inner,), jnp.int32),
        ],
        out_shape=[
            jax.ShapeDtypeStruct((slots, heads, rows, HD), jnp.bfloat16),
            jax.ShapeDtypeStruct((slots, heads, PAD, length), jnp.float32),
        ],
        compiler_params=pltpu.CompilerParams(vmem_limit_bytes=60 * MIB),
        name="attend",
    )(owners, facts, qg, kvg, kvg)


def finish_kernel(
    cfg, outs, lses, own_out, own_lse, wo,
    result,
    obuf, lbuf, vo, square, context, psend, precv,
    wsem, lsem, osend, orecv, ssend, srecv, xsend, xrecv,
):
    tps, inner, split, slots, kv_heads, group = cfg
    half = kv_heads // split
    length, width = result.shape
    tile = 512 if width % 512 == 0 else width
    req, tp = lax.axis_index("req"), lax.axis_index("tp")
    part = lax.rem(req, split)

    load = pltpu.make_async_copy(wo, vo, wsem.at[0])
    load.start()
    greet(req, tp, slots[1:], range(1, tps))
    short = length // PIECES
    step = group * short
    order = range(len(slots) - 1, 0, -1)
    stats = [
        pltpu.make_async_remote_copy(
            src_ref=lses.at[n],
            dst_ref=lbuf.at[n],
            send_sem=ssend.at[n - 1],
            recv_sem=srecv.at[n - 1],
            device_id=(flip(req, slots[n]), tp),
            device_id_type=MESH,
        )
        for n in order
    ]

    def answer_of(n, piece):
        rows = pl.ds(piece * step, step)
        return pltpu.make_async_remote_copy(
            src_ref=outs.at[n, :, rows],
            dst_ref=obuf.at[n, :, rows],
            send_sem=osend.at[piece, n - 1],
            recv_sem=orecv.at[piece, n - 1],
            device_id=(flip(req, slots[n]), tp),
            device_id_type=MESH,
        )

    answers = [[answer_of(n, piece) for n in order] for piece in range(PIECES)]
    for copy in stats + answers[0]:
        copy.start()
    keeps = [
        pltpu.make_async_copy(outs.at[0], obuf.at[0], lsem.at[0]),
        pltpu.make_async_copy(lses.at[0], lbuf.at[0], lsem.at[1]),
    ]
    for keep in keeps:
        keep.start()
    for copy in keeps + stats:
        copy.wait()

    square[...] = jnp.zeros_like(square)
    terms = OUTER + 1
    for sub in range(split):
        which = flip(part, sub)
        for g in range(half):
            parts = [lbuf[so * split + sub, g] for so in range(OUTER)]
            own = own_lse[which]
            parts.append(own[g * group : (g + 1) * group])
            parts = [p[:group] for p in parts]
            top = functools.reduce(jnp.maximum, parts)
            shares = [jnp.exp(p - top) for p in parts]
            whole = functools.reduce(jnp.add, shares)
            for j, share in enumerate(shares):
                at = ((sub * half + g) * terms + j) * group
                square[at : at + group] = share / whole
    columns = jnp.transpose(square[...])
    def product(target, piece, n):
        at = pl.multiple_of(target * width + n * tile, 128)
        return jnp.dot(
            context[piece * short : (piece + 1) * short],
            vo[:, pl.ds(at, tile)],
            preferred_element_type=jnp.float32,
        ).astype(jnp.bfloat16)

    swaps = []
    for piece in range(PIECES):
        slot_rows = slice(piece * short, (piece + 1) * short)
        if piece + 1 < PIECES:
            for copy, later in zip(answers[piece], answers[piece + 1]):
                copy.wait_send()
                later.start()
            for copy in answers[piece]:
                copy.wait_recv()
        else:
            for copy in answers[piece]:
                copy.wait()
        for sub in range(split):
            which = flip(part, sub)
            for g in range(half):
                for h in range(group):
                    total = jnp.zeros((short, HD), jnp.float32)
                    first = piece * step + h * short
                    rows = slice(first, first + short)
                    for j in range(terms):
                        at = ((sub * half + g) * terms + j) * group + h
                        if j < OUTER:
                            term = obuf[j * split + sub, g, rows]
                        else:
                            term = own_out[which, g, rows]
                        total = total + term.astype(jnp.float32) * columns[slot_rows, at : at + 1]
                    to = pl.multiple_of(((which * half + g) * group + h) * HD, HD)
                    context[slot_rows, pl.ds(to, HD)] = total.astype(jnp.bfloat16)
        if piece == 0:
            load.wait()
        for k in range(1, tps):
            for n in range(width // tile):
                psend[k - 1, slot_rows, n * tile : (n + 1) * tile] = product(
                    flip(tp, k), piece, n
                )
            swap = pltpu.make_async_remote_copy(
                src_ref=psend.at[k - 1, pl.ds(piece * short, short)],
                dst_ref=precv.at[k - 1, pl.ds(piece * short, short)],
                send_sem=xsend.at[piece, k - 1],
                recv_sem=xrecv.at[piece, k - 1],
                device_id=(req, flip(tp, k)),
                device_id_type=MESH,
            )
            swap.start()
            swaps.append((k, slot_rows, swap))
        for n in range(width // tile):
            result[slot_rows, n * tile : (n + 1) * tile] = product(tp, piece, n).astype(
                jnp.float32
            )
    for k, slot_rows, swap in swaps:
        swap.wait()
        result[slot_rows] += precv[k - 1, slot_rows].astype(jnp.float32)


def finish(outs, lses, own_out, own_lse, wo, cfg):
    tps, inner, split, slots, kv_heads, group = cfg
    length = lses.shape[-1]
    width = wo.shape[1] // tps
    vmem = pl.BlockSpec(memory_space=pltpu.VMEM)
    hbm = pl.BlockSpec(memory_space=pl.ANY)
    bf16, f32 = jnp.bfloat16, jnp.float32
    dma = pltpu.SemaphoreType.DMA
    return pl.pallas_call(
        functools.partial(finish_kernel, cfg),
        in_specs=[hbm, hbm, vmem, vmem, hbm],
        out_specs=vmem,
        out_shape=jax.ShapeDtypeStruct((length, width), f32),
        scratch_shapes=[
            pltpu.VMEM(outs.shape, bf16),
            pltpu.VMEM(lses.shape, f32),
            pltpu.VMEM(wo.shape, bf16),
            pltpu.VMEM((128, length), f32),
            pltpu.VMEM((length, wo.shape[0]), bf16),
            pltpu.VMEM((tps - 1, length, width), bf16),
            pltpu.VMEM((tps - 1, length, width), bf16),
            dma((1,)),
            dma((2,)),
            dma((PIECES, len(slots) - 1)),
            dma((PIECES, len(slots) - 1)),
            dma((len(slots) - 1,)),
            dma((len(slots) - 1,)),
            dma((PIECES, tps - 1)),
            dma((PIECES, tps - 1)),
        ],
        compiler_params=pltpu.CompilerParams(
            collective_id=1, has_side_effects=True, vmem_limit_bytes=60 * MIB
        ),
        name="finish",
    )(outs, lses, own_out, own_lse, wo)


def shards(
    hidden_in,
    norm_gain,
    q_weight,
    q_bias,
    k_weight,
    k_bias,
    v_weight,
    v_bias,
    o_weight,
    prefix_kv,
    suffix_len,
    req_prefix,
    block_owner,
):
    length = hidden_in.shape[0]
    devices = lax.axis_size("req")
    tps = lax.axis_size("tp")
    owned = devices // NPREF
    block = prefix_kv.shape[0]
    kv_heads = k_weight.shape[1] // HD
    group = q_weight.shape[1] // k_weight.shape[1]
    inner = devices // OUTER
    split = 2 if kv_heads % 2 == 0 else 1
    slots = tuple(so * inner + sub for so in range(OUTER) for sub in range(split))
    cfg = (tps, inner, split, slots, kv_heads, group)

    facts = jnp.concatenate([req_prefix, jnp.broadcast_to(suffix_len, (7,))])
    facts = jnp.broadcast_to(facts[:, None], (8, 128))
    kvs = prefix_kv.reshape(block, 2 * kv_heads * HD)
    params = lax.optimization_barrier(jnp.concatenate([norm_gain, q_bias, k_bias, v_bias]))
    params = jnp.broadcast_to(params.astype(jnp.float32)[None, :], (8, params.shape[0]))
    cosine, sine = tables(block * owned + np.arange(length))
    qg, kvg, facts, own_out, own_lse = project(
        hidden_in, params, jnp.asarray(cosine), jnp.asarray(sine), facts, kvs,
        q_weight, k_weight, v_weight, cfg,
    )
    outs, lses = attend(block_owner, facts, qg, kvg, group)
    summed = finish(outs, lses, own_out, own_lse, o_weight, cfg)
    valid = jnp.arange(length, dtype=jnp.int32) < suffix_len[0]
    return jnp.where(valid[:, None], summed, jnp.float32(0.0)).astype(jnp.bfloat16)


def solution(mesh):
    placed = (
        P("req", "tp"),
        P("tp"),
        P(None, "tp"),
        P("tp"),
        P(None, "tp"),
        P("tp"),
        P(None, "tp"),
        P("tp"),
        P("tp", None),
        P("req", None, "tp"),
        P("req"),
        P("req"),
        P(),
    )
    return jax.shard_map(
        shards, mesh=mesh, in_specs=placed, out_specs=P("req", "tp"), check_vma=False
    )
```
